32 devices in a mesh: ens: 2 (over x), lon: 16 (over z, y, core).
Axes of the slice: x: 2, y: 2, z: 4, core: 2. Of those that a mesh axis runs over, the one named last changes fastest.
Arguments:
- tracer: float32 [4, 256, 75, 256], P(None, 'lon', None, 'ens'), parts along dimension 3, may hold values from -6 to 6
- east_speed: float32 [256, 75, 256], P('lon', None, 'ens'), parts along dimension 2, may hold values from -0.25 to 0.25
- north_speed: float32 [256, 75, 256], P('lon', None, 'ens'), parts along dimension 2, may hold values from -0.25 to 0.25
- diffusivity: float32 [256, 75, 256], P('lon', None, 'ens'), parts along dimension 2, may hold values from 0.02 to 0.2
- mixing: float32 [256, 75, 256], P('lon', None, 'ens'), parts along dimension 2, may hold values from 0.05 to 5
- thickness: float32 [256, 75, 256], P('lon', None, 'ens'), parts along dimension 2, may hold values from 0.5 to 2
- depth_levels: int32 [256, 256], P('lon', 'ens'), parts along dimension 1, may hold values from 0 to 75
- air_flux: float32 [8, 4096], P('ens', 'lon'), parts along dimension 0, may hold values from -6 to 6
- margin_tile: int32 [32768, 1], P(('ens', 'lon')), parts along dimension 0, may hold values from 0 to 15; in each aligned block of 1024 rows (0 to 1023, 1024 to 2047, ...) at most 64 rows name the same one
- margin_source: int32 [32768], P(('ens', 'lon')), parts along dimension 0, may hold values from 0 to 255
- margin_cell: int32 [32768], P(('ens', 'lon')), parts along dimension 0, may hold values from 0 to 2047
- margin_weight: float32 [32768], P(('ens', 'lon')), parts along dimension 0, may hold values from 0.2 to 1
Outputs:
- tracer_next: float32 [4, 256, 75, 256], P(None, 'lon', None, 'ens'), parts along dimension 3
The draws below stay inside these ranges and needn't reach their ends.
There are 2 independent parts, one for each index of `ens`. The reference program is written for one: setup_inputs(seed, part) draws one part's arguments, and reference() takes and returns one part's arrays. A program takes and returns all parts, laid end to end along the dimension named above; each array names one. Nothing has to cross between parts.
Inputs may be any that keep to these rules, and one draw needn't show every extreme that they name: `margin_tile`: the rows of one tile name each ocean tile at most 64 times.
All inputs are finite; a program needn't handle non-finite values.
Results may differ from the reference program's by a relative error of at most 0.00002.
Values sent between devices are 32-bit elements; how exact they have to be, the bound alone decides.
No kernel may reach another device: no remote copies, remote signals or barrier semaphores. Data moves between devices by JAX's collectives and lax.ppermute only.
A program may use at most 192 MiB of HBM per device.

```python
import math
import jax
import jax.numpy as jnp
import numpy as np

LX = 16
NY = 128
NZ = 75
TRACERS = 4
ACELL_DEV = 256
OVL_DEV = 1024
CAP = 64
NX = 256
ACELLS = 4096
OVL = 16384
N_LON = 16


def touch_ends(entries, own_key, least, top_value):
    shape = entries.shape
    place = [jax.random.randint(jax.random.fold_in(own_key, axis), (), 0, shape[axis]) for axis in range(len(shape))]
    entries = entries.at[tuple(place)].set(least)
    longest = shape.index(max(shape))
    place[longest] = (place[longest] + 1) % shape[longest]
    return entries.at[tuple(place)].set(top_value)


def block_scale(key, extent, cuts, least, high):
    loudness, own = 1.0, jax.random.fold_in(key, 6)
    for position, parts in cuts:
        draws = jnp.exp(jax.random.uniform(jax.random.fold_in(own, position), (parts,), jnp.float32, least / len(cuts), high / len(cuts)))
        loudness = loudness * jnp.repeat(draws, extent[position] // parts).reshape([-1 if axis == position else 1 for axis in range(len(extent))])
    return loudness


def shared_out(key, own, number, rows, amount, top, bound, lean):
    ranking = jax.random.permutation(key, amount)
    heavy_load, ordinary = portions_of(amount, rows * top, bound, lean, True), portions_of(amount, rows * top, bound, lean, False)
    places = jnp.arange(amount)

    def named(lengths, rotation):
        used = int((lengths > 0).sum())
        fixed = max(1, used // 4)
        shifted = fixed + (places - fixed + rotation * (used - fixed)) % max(1, amount - fixed)
        return jnp.zeros((amount,), jnp.int32).at[ranking[jnp.where(places < fixed, places, shifted)]].set(jnp.asarray(lengths, jnp.int32))

    lengths = jnp.where(number % 4 == 0, named(heavy_load, number // 4), named(ordinary, number - number // 4 - 1))
    mixed = jax.random.permutation(jax.random.fold_in(own, 3), amount)
    giver, sink = mixed[0:amount // 2 * 2:2], mixed[1:amount // 2 * 2:2]
    margin = jnp.minimum(lengths[giver] - 1, bound - lengths[sink]) // 2
    margin = jnp.where((giver == ranking[0]) | (sink == ranking[0]) | (lengths[sink] == 0), 0, jnp.maximum(margin, 0))
    shifted = jax.random.randint(jax.random.fold_in(own, 4), (amount // 2,), 0, 1 << 20) % (margin + 1)
    lengths = lengths.at[giver].add(-shifted).at[sink].add(shifted)
    items = jnp.searchsorted(jnp.cumsum(lengths), jnp.arange(rows * top), side="right").astype(jnp.int32)
    listing = items.reshape(top, rows).T
    listing = listing[jax.random.permutation(jax.random.fold_in(own, 1), rows)]
    rotation = jax.random.randint(jax.random.fold_in(own, 2), (rows, 1), 0, top)
    return jnp.take_along_axis(listing, (jnp.arange(top)[None, :] + rotation) % top, axis=1)


def portions_of(number_of, total, most, slope, full):
    loads = [(1 << 20) // math.isqrt(rank ** slope) + 1 for rank in range(1, number_of + 1)]
    largest = most if full else min(most, max(-(-total // number_of), total * loads[0] // sum(loads)))
    least = 1 if total - largest >= number_of - 1 else 0
    given, surplus = [largest] + [least] * (number_of - 1), total - largest - least * (number_of - 1)
    while surplus > 0:
        candidates = [i for i in range(1, number_of) if given[i] < largest] or [i for i in range(1, number_of) if given[i] < most]
        pool, left = sum([loads[i] for i in candidates]), surplus
        for i in candidates:
            extra = min(most - given[i], max(1, left * loads[i] // pool), surplus)
            given[i] = given[i] + extra
            surplus = surplus - extra
    return np.array(given)


def bell_draw(own_key, dims, deviation, most, pieces=(), kind=jnp.bfloat16):
    result = deviation * jax.random.normal(own_key, dims, jnp.float32)
    if pieces:
        result = result * block_scale(own_key, dims, pieces, -0.22, 0.18)
    return jnp.clip(result, -most, most).astype(kind)


def setup_inputs(seed: int = 0, part: int = 0) -> dict:
    keys = jax.random.split(jax.random.key(seed), 13)
    own_keys = jax.random.split(jax.random.fold_in(keys[12], part), 13)
    tracer = bell_draw(own_keys[0], (TRACERS, NX, NZ, NY), 1.0, 6.0, ((1, 16),), jnp.float32)
    east_speed = jnp.clip(jax.random.uniform(own_keys[1], (NX, NZ, NY), jnp.float32, -0.25, 0.25) * block_scale(own_keys[1], (NX, NZ, NY), ((0, 16),), -0.4, 0.0), -0.25, 0.25)
    north_speed = jnp.clip(jax.random.uniform(own_keys[2], (NX, NZ, NY), jnp.float32, -0.25, 0.25) * block_scale(own_keys[2], (NX, NZ, NY), ((0, 16),), -0.4, 0.0), -0.25, 0.25)
    diffusivity = jnp.clip(jnp.exp(math.log(0.2) - 2.3025851 * jax.random.uniform(own_keys[3], (NX, NZ, NY), jnp.float32) ** block_scale(own_keys[3], (NX, NZ, NY), ((0, 16),), -0.2, 0.2)), 0.02, 0.2)
    mixing = jnp.clip(jnp.exp(math.log(5.0) - 4.6051702 * jax.random.uniform(own_keys[4], (NX, NZ, NY), jnp.float32) ** block_scale(own_keys[4], (NX, NZ, NY), ((0, 16),), -0.2, 0.2)), 0.05, 5.0)
    thickness = jnp.clip(jnp.exp(math.log(2.0) - 1.3862944 * jax.random.uniform(own_keys[5], (NX, NZ, NY), jnp.float32) ** block_scale(own_keys[5], (NX, NZ, NY), ((0, 16),), -0.2, 0.2)), 0.5, 2.0)
    depth_levels = touch_ends(jax.random.randint(own_keys[6], (NX, NY), 0, NZ + 1), jax.random.fold_in(own_keys[6], 1), 0, NZ).astype(jnp.int32)
    air_flux = bell_draw(own_keys[7], (TRACERS, ACELLS), 1.0, 6.0, ((1, 16),), jnp.float32)
    margin_tile_keys = jax.random.split(jax.random.fold_in(own_keys[8], 1), OVL // OVL_DEV)
    margin_tile_turns = jax.random.permutation(jax.random.fold_in(own_keys[8], 3), OVL // OVL_DEV)
    margin_tile = jax.vmap(lambda own, number: shared_out(jax.random.fold_in(own_keys[8], 2), own, number, OVL_DEV, N_LON, 1, CAP, 2))(margin_tile_keys, margin_tile_turns).reshape((OVL, 1))
    margin_source = touch_ends(jax.random.randint(own_keys[9], (OVL,), 0, ACELL_DEV), jax.random.fold_in(own_keys[9], 1), 0, ACELL_DEV - 1).astype(jnp.int32)
    margin_cell = touch_ends(jax.random.randint(own_keys[10], (OVL,), 0, LX * NY), jax.random.fold_in(own_keys[10], 1), 0, (LX * NY) - 1).astype(jnp.int32)
    margin_weight = jnp.clip(0.2 + 0.8 * jax.random.uniform(own_keys[11], (OVL,), jnp.float32) ** block_scale(own_keys[11], (OVL,), ((0, 16),), -0.2, 0.2), 0.2, 1.0)
    return {"tracer": tracer, "east_speed": east_speed, "north_speed": north_speed, "diffusivity": diffusivity, "mixing": mixing, "thickness": thickness, "depth_levels": depth_levels, "air_flux": air_flux, "margin_tile": margin_tile, "margin_source": margin_source, "margin_cell": margin_cell, "margin_weight": margin_weight}


def face_flux(speed, kappa_near, kappa_far, open_face, near, far):
    return open_face * (jnp.maximum(speed, 0.0) * near + jnp.minimum(speed, 0.0) * far + 0.5 * (kappa_near + kappa_far) * (near - far))


def mix_columns(stepped, mixing, thickness, wet_mask, surface):
    levels = stepped.shape[2]
    wet_below = jnp.concatenate([wet_mask[:, 1:], jnp.zeros_like(wet_mask[:, :1])], axis=1)
    thickness_below = jnp.concatenate([thickness[:, 1:], thickness[:, -1:]], axis=1)
    coupling = mixing * wet_below / (0.5 * (thickness + thickness_below))
    prior_coupling = jnp.zeros_like(thickness[:, 0])
    prior_gain = jnp.zeros_like(thickness[:, 0])
    prior_value = jnp.zeros_like(stepped[:, :, 0])
    gain_list = []
    value_list = []
    for level_index in range(levels):
        here_coupling = coupling[:, level_index]
        here_thickness = thickness[:, level_index]
        pivot_value = here_thickness + here_coupling + prior_coupling - prior_coupling * prior_gain
        right_side = here_thickness * stepped[:, :, level_index]
        if level_index == 0:
            right_side = right_side + wet_mask[:, 0] * surface
        prior_value = (right_side + prior_coupling * prior_value) / pivot_value
        prior_gain = here_coupling / pivot_value
        prior_coupling = here_coupling
        gain_list.append(prior_gain)
        value_list.append(prior_value)
    solved = [value_list[-1]]
    for level_index in range(levels - 2, -1, -1):
        solved.append(value_list[level_index] + gain_list[level_index] * solved[-1])
    return jnp.stack(solved[::-1], axis=2)


def reference(tracer, east_speed, north_speed, diffusivity, mixing, thickness, depth_levels, air_flux, margin_tile, margin_source, margin_cell, margin_weight):
    level_ids = jnp.arange(NZ).astype(jnp.int32)
    wet_mask = (level_ids[None, :, None] < depth_levels[:, None, :]).astype(jnp.float32)
    east_flux = face_flux(east_speed[None], diffusivity[None], jnp.roll(diffusivity, -1, axis=0)[None], (wet_mask * jnp.roll(wet_mask, -1, axis=0))[None], tracer, jnp.roll(tracer, -1, axis=1))
    zonal_change = east_flux - jnp.roll(east_flux, 1, axis=1)
    mirror_tracer = jnp.flip(tracer[:, :, :, -1], axis=1)
    mirror_speed = jnp.flip(north_speed[:, :, -1], axis=0)
    mirror_kappa = jnp.flip(diffusivity[:, :, -1], axis=0)
    mirror_wet = jnp.flip(wet_mask[:, :, -1], axis=0)
    fold_flux = face_flux((0.5 * (north_speed[:, :, -1] - mirror_speed))[None], diffusivity[None, :, :, -1], mirror_kappa[None], (wet_mask[:, :, -1] * mirror_wet)[None], tracer[:, :, :, -1], mirror_tracer)
    inner_flux = face_flux(north_speed[None, :, :, :-1], diffusivity[None, :, :, :-1], diffusivity[None, :, :, 1:], (wet_mask[:, :, :-1] * wet_mask[:, :, 1:])[None], tracer[:, :, :, :-1], tracer[:, :, :, 1:])
    north_flux = jnp.concatenate([inner_flux, fold_flux[..., None]], axis=3)
    south_flux = jnp.concatenate([jnp.zeros_like(inner_flux[..., :1]), inner_flux], axis=3)
    stepped = tracer - zonal_change - (north_flux - south_flux)
    owner = (jnp.arange(OVL) // OVL_DEV).astype(jnp.int32)
    source = owner * ACELL_DEV + margin_source
    payload = margin_weight[None, :] * jnp.take(air_flux, source, axis=1)
    target = margin_tile[:, 0] * (LX * NY) + margin_cell
    surface = jnp.zeros((TRACERS, NX * NY), jnp.float32).at[:, target].add(payload).reshape(TRACERS, NX, NY)
    return mix_columns(stepped, mixing, thickness, wet_mask, surface)
```

```python
import functools

import jax
import jax.numpy as jnp
from jax import lax
from jax.experimental import pallas as pl
from jax.experimental.pallas import tpu as pltpu
from jax.sharding import PartitionSpec as P

CAP = 64
HALF = 8
LANES = 128
F32 = jnp.float32


def chunk_of(levels):
    return max(c for c in range(1, 16) if levels % c == 0)


def thirds(x):
    high = x.astype(jnp.bfloat16)
    rest = x - high.astype(F32)
    mid = rest.astype(jnp.bfloat16)
    low = (rest - mid.astype(F32)).astype(jnp.bfloat16)
    return high, mid, low


def lane_ids(rows):
    return lax.broadcasted_iota(jnp.int32, (rows, LANES), 1)


def row_ids(rows):
    return lax.broadcasted_iota(jnp.int32, (rows, LANES), 0)


def dot_nt(a, b):
    return lax.dot_general(a, b, (((1,), (1,)), ((), ())), preferred_element_type=F32)


def dot_nn(a, b):
    return lax.dot_general(a, b, (((1,), (0,)), ((), ())), preferred_element_type=F32)


def make_messages(tiles, air_ref, tile_ref, source_ref, cell_ref, weight_ref, msg_ref):
    count, air_cells = air_ref.shape
    chunks = tile_ref.shape[0]
    one, zero = jnp.ones((), F32), jnp.zeros((), F32)
    rows = [slice(c, c + 1) for c in range(chunks)]
    owns = [
        jnp.broadcast_to(tile_ref[r, :], (tiles, LANES)) == row_ids(tiles) for r in rows
    ]
    owned = jnp.concatenate([jnp.where(o, one, zero) for o in owns], axis=0).astype(jnp.bfloat16)
    earlier = jnp.where(row_ids(LANES) < lane_ids(LANES), one, zero).astype(jnp.bfloat16)
    prior = dot_nn(owned, earlier)
    total = dot_nn(owned, jnp.ones((LANES, LANES), jnp.bfloat16))
    air_parts = jnp.concatenate(
        [p.astype(F32) for p in thirds(air_ref[...])], axis=0
    ).astype(jnp.bfloat16)
    carry = jnp.zeros((tiles, LANES), F32)
    slots, parts = [], []
    for c in range(chunks):
        span = slice(c * tiles, (c + 1) * tiles)
        slots.append(
            jnp.sum(jnp.where(owns[c], prior[span] + carry, zero), axis=0, keepdims=True)
        )
        carry = carry + total[span]
        picked = jnp.broadcast_to(source_ref[rows[c], :], (air_cells, LANES)) == row_ids(air_cells)
        taken = dot_nn(air_parts, jnp.where(picked, one, zero).astype(jnp.bfloat16))
        flux = taken[:count] + taken[count : 2 * count] + taken[2 * count : 3 * count]
        payload = weight_ref[rows[c], :] * flux
        record = jnp.concatenate(
            [
                payload,
                cell_ref[rows[c], :].astype(F32),
                jnp.zeros((HALF - count - 1, LANES), F32),
            ],
            axis=0,
        )
        parts.append([p.astype(F32) for p in thirds(record)])
    slot_hot = jnp.concatenate(
        [
            jnp.where(
                jnp.broadcast_to(s.astype(jnp.int32), (LANES, LANES)) == row_ids(LANES), one, zero
            ).astype(jnp.bfloat16)
            for s in slots
        ],
        axis=1,
    )
    out = jnp.zeros((tiles * HALF, LANES), F32)
    for part in range(3):
        spread = jnp.concatenate(
            [
                jnp.concatenate(
                    [
                        jnp.where(
                            jnp.broadcast_to(tile_ref[rows[c], :], (HALF, LANES)) == d,
                            parts[c][part],
                            zero,
                        )
                        for d in range(tiles)
                    ],
                    axis=0,
                ).astype(jnp.bfloat16)
                for c in range(chunks)
            ],
            axis=1,
        )
        out = out + dot_nt(spread, slot_hot)
    msg_ref[...] = out.reshape(tiles, HALF, LANES)


def pack_kernel(
    levels,
    tiles,
    tracer_ref,
    east_ref,
    north_ref,
    kappa_ref,
    depth_ref,
    air_ref,
    tile_ref,
    source_ref,
    cell_ref,
    weight_ref,
    up_ref,
    down_ref,
    mirror_ref,
    msg_ref,
    column_ref,
):
    step = pl.program_id(0)
    count, chunk, cells, _ = tracer_ref.shape
    fields = count + 2
    lane = lane_ids(cells)

    @pl.when(step == 0)
    def _():
        depth = depth_ref[...].astype(F32)
        up_ref[fields * levels : fields * levels + 1, :] = depth[cells - 1 : cells]
        down_ref[(fields - 1) * levels : (fields - 1) * levels + 1, :] = depth[0:1]
        column_ref[...] = jnp.zeros_like(column_ref)
        column_ref[0] = jnp.where(lane == levels, pltpu.roll(depth, levels + 1, 1), 0.0)
        make_messages(tiles, air_ref, tile_ref, source_ref, cell_ref, weight_ref, msg_ref)

    columns = [column_ref[f] for f in range(fields)]
    for here in range(chunk):
        k = step * chunk + here
        slabs = [tracer_ref[n, here] for n in range(count)] + [north_ref[here], kappa_ref[here]]
        for f in range(fields):
            columns[f] = jnp.where(lane == k, pltpu.roll(slabs[f], k + 1, 1), columns[f])
            if f < count:
                up_ref[pl.ds(f * levels + k, 1), :] = slabs[f][cells - 1 : cells]
                down_ref[pl.ds(f * levels + k, 1), :] = slabs[f][0:1]
        up_ref[pl.ds(count * levels + k, 1), :] = east_ref[here][HALF - 1 : HALF]
        up_ref[pl.ds((count + 1) * levels + k, 1), :] = slabs[count + 1][cells - 1 : cells]
        down_ref[pl.ds(count * levels + k, 1), :] = slabs[count + 1][0:1]
    for f in range(fields):
        column_ref[f] = columns[f]

    @pl.when(step == pl.num_programs(0) - 1)
    def _():
        for f in range(fields):
            for i in range(cells):
                mirror_ref[f * cells + cells - 1 - i : f * cells + cells - i, :] = columns[f][
                    i : i + 1
                ]


def pack(tiles, tracer, east, north, kappa, depth, air, tile, source, cell, weight):
    count, levels, cells, lat = tracer.shape
    fields = count + 2
    chunk = chunk_of(levels)
    whole = lambda x: pl.BlockSpec(x.shape, lambda s, nd=x.ndim: (0,) * nd)
    level = lambda s: (s, 0, 0)
    out = [
        jax.ShapeDtypeStruct((-(-(fields * levels + 1) // HALF) * HALF, lat), F32),
        jax.ShapeDtypeStruct((-(-((fields - 1) * levels + 1) // HALF) * HALF, lat), F32),
        jax.ShapeDtypeStruct((fields * cells, LANES), F32),
        jax.ShapeDtypeStruct((tiles, HALF, LANES), F32),
    ]
    return pl.pallas_call(
        functools.partial(pack_kernel, levels, tiles),
        grid=(levels // chunk,),
        out_shape=out,
        in_specs=[
            pl.BlockSpec((count, chunk, cells, lat), lambda s: (0, s, 0, 0)),
            pl.BlockSpec((chunk, HALF, lat), lambda s: (s, cells // HALF - 1, 0)),
            pl.BlockSpec((chunk, cells, lat), level),
            pl.BlockSpec((chunk, cells, lat), level),
        ]
        + [whole(x) for x in (depth, air, tile, source, cell, weight)],
        out_specs=[whole(o) for o in out],
        scratch_shapes=[pltpu.VMEM((fields, cells, LANES), F32)],
        compiler_params=pltpu.CompilerParams(vmem_limit_bytes=24 << 20),
        cost_estimate=pl.CostEstimate(flops=10**7, bytes_accessed=4 * 10**6, transcendentals=0),
        name="pack",
    )(tracer, east, north, kappa, depth, air, tile, source, cell, weight)


def gather_surface(count, cells, lat, received_ref):
    tiles = received_ref.shape[0]
    shift = lat.bit_length() - 1
    values, spots = [[], [], []], []
    one, zero = jnp.ones((), F32), jnp.zeros((), F32)
    left, right = [[], [], []], []
    for t in range(tiles):
        block = received_ref[t]
        cell = block[count : count + 1].astype(jnp.int32)
        row = jnp.broadcast_to(lax.shift_right_logical(cell, shift), (cells, LANES))
        col = jnp.broadcast_to(cell & (lat - 1), (lat, LANES))
        right.append(jnp.where(col == row_ids(lat), one, zero).astype(jnp.bfloat16))
        hit = row == row_ids(cells)
        for p, part in enumerate(thirds(block)):
            part = part.astype(F32)
            left[p].append(
                jnp.concatenate(
                    [
                        jnp.where(hit, jnp.broadcast_to(part[n : n + 1], (cells, LANES)), zero)
                        for n in range(count)
                    ],
                    axis=0,
                ).astype(jnp.bfloat16)
            )
    spread = jnp.concatenate(right, axis=1)
    return sum(dot_nt(jnp.concatenate(left[p], axis=1), spread) for p in range(3))


def step_kernel(
    levels,
    tracer_ref,
    east_ref,
    north_ref,
    kappa_ref,
    mixing_ref,
    thick_ref,
    depth_ref,
    west_ref,
    far_ref,
    mirror_ref,
    received_ref,
    out_ref,
    value_ref,
    gain_ref,
    rhs_ref,
    thickness_ref,
    coupling_ref,
    limit_ref,
):
    step = pl.program_id(0)
    count, chunk, cells, lat = tracer_ref.shape
    blocks = pl.num_programs(0) // 2
    halves = cells // HALF
    fields = count + 2
    row8 = row_ids(HALF)
    lane8 = lane_ids(HALF)
    top = lane8 == lat - 1
    bottom = lane8 == 0
    first = row8 == 0
    last = row8 == HALF - 1
    hs = [slice(h * HALF, (h + 1) * HALF) for h in range(halves)]

    def from_east(parts, halo):
        turned = [pltpu.roll(p, HALF - 1, 0) for p in parts]
        return [
            jnp.where(last, turned[h + 1] if h + 1 < halves else halo, turned[h])
            for h in range(halves)
        ]

    def from_west(parts, halo):
        turned = [pltpu.roll(p, 1, 0) for p in parts]
        return [
            jnp.where(first, turned[h - 1] if h > 0 else halo, turned[h]) for h in range(halves)
        ]

    def row_of(ref, index):
        return jnp.broadcast_to(ref[pl.ds(index, 1), :], (HALF, lat))

    def mirrored(field, h, k):
        spot = field * cells + h * HALF
        return pltpu.roll(mirror_ref[spot : spot + HALF, :], lat - 1 - k, 1)

    @pl.when(step == 0)
    def _():
        depth = [depth_ref[s, :].astype(F32) for s in hs]
        east = from_east(depth, row_of(far_ref, (fields - 1) * levels))
        for h in range(halves):
            limit_ref[0, hs[h], :] = jnp.minimum(depth[h], east[h])
            north = jnp.where(top, mirrored(0, h, levels), pltpu.roll(depth[h], lat - 1, 1))
            limit_ref[1, hs[h], :] = jnp.minimum(depth[h], north)
            limit_ref[2, hs[h], :] = depth[h]
        limit_ref[3, 0:HALF, :] = jnp.minimum(
            jnp.broadcast_to(depth[0][0:1], (HALF, lat)), row_of(west_ref, fields * levels)
        )
        rhs_ref[...] = jnp.zeros_like(rhs_ref)
        thickness_ref[...] = jnp.ones_like(thickness_ref)
        coupling_ref[...] = jnp.zeros_like(coupling_ref)
        value_ref[:, levels] = jnp.zeros((count, cells, lat), F32)
        gain_ref[levels] = jnp.zeros((cells, lat), F32)

    @pl.when(step < blocks)
    def _():
        block = blocks - 1 - step
        limit_east = [limit_ref[0, s, :] for s in hs]
        limit_north = [limit_ref[1, s, :] for s in hs]
        limit_here = [limit_ref[2, s, :] for s in hs]
        limit_west = limit_ref[3, 0:HALF, :]
        rhs = [[rhs_ref[n, s, :] for s in hs] for n in range(count)]
        thick_below = [thickness_ref[s, :] for s in hs]
        coupling_below = [coupling_ref[s, :] for s in hs]
        held = block * chunk + chunk
        value = [[value_ref[n, jnp.minimum(held + 1, levels), s, :] for s in hs] for n in range(count)]
        gain = [gain_ref[jnp.minimum(held + 1, levels), s, :] for s in hs]
        for here in range(chunk - 1, -1, -1):
            k = block * chunk + here
            level = k.astype(F32)
            kappa = [kappa_ref[here, s, :] for s in hs]
            speed = [east_ref[here, s, :] for s in hs]
            kappa_east = from_east(kappa, row_of(far_ref, count * levels + k))
            near_e, far_e = [], []
            for h in range(halves):
                mean = 0.5 * (kappa[h] + kappa_east[h])
                open_face = limit_east[h] > level
                near_e.append(jnp.where(open_face, jnp.maximum(speed[h], 0.0) + mean, 0.0))
                far_e.append(jnp.where(open_face, jnp.minimum(speed[h], 0.0) - mean, 0.0))
            speed_w = row_of(west_ref, count * levels + k)
            mean = 0.5 * (row_of(west_ref, (count + 1) * levels + k) + jnp.broadcast_to(kappa[0][0:1], (HALF, lat)))
            open_face = limit_west > level
            near_w = jnp.where(open_face, jnp.maximum(speed_w, 0.0) + mean, 0.0)
            far_w = jnp.where(open_face, jnp.minimum(speed_w, 0.0) - mean, 0.0)
            near_n, far_n = [], []
            for h in range(halves):
                speed_n = north_ref[here, hs[h], :]
                speed_n = jnp.where(top, 0.5 * (speed_n - mirrored(count, h, k)), speed_n)
                kappa_n = jnp.where(
                    top, mirrored(count + 1, h, k), pltpu.roll(kappa[h], lat - 1, 1)
                )
                mean = 0.5 * (kappa[h] + kappa_n)
                open_face = limit_north[h] > level
                near_n.append(jnp.where(open_face, jnp.maximum(speed_n, 0.0) + mean, 0.0))
                far_n.append(jnp.where(open_face, jnp.minimum(speed_n, 0.0) - mean, 0.0))
            thick = [thick_ref[here, s, :] for s in hs]
            coupling, scale = [], []
            for h in range(halves):
                wet_below = limit_here[h] > level + 1.0
                here_c = jnp.where(
                    wet_below,
                    2.0 * mixing_ref[here, hs[h], :] / (thick[h] + thick_below[h]),
                    0.0,
                )
                coupling.append(here_c)
                pivot = thick_below[h] + here_c + coupling_below[h] - coupling_below[h] * gain[h]
                scale.append(1.0 / pivot)
            for h in range(halves):
                gain[h] = coupling[h] * scale[h]
                gain_ref[k + 1, hs[h], :] = gain[h]
            for n in range(count):
                cell = [tracer_ref[n, here, s, :] for s in hs]
                cell_east = from_east(cell, row_of(far_ref, n * levels + k))
                flux_e = [near_e[h] * cell[h] + far_e[h] * cell_east[h] for h in range(halves)]
                flux_in = near_w * row_of(west_ref, n * levels + k) + far_w * jnp.broadcast_to(
                    cell[0][0:1], (HALF, lat)
                )
                flux_w = from_west(flux_e, flux_in)
                for h in range(halves):
                    cell_north = jnp.where(
                        top, mirrored(n, h, k), pltpu.roll(cell[h], lat - 1, 1)
                    )
                    flux_n = near_n[h] * cell[h] + far_n[h] * cell_north
                    flux_s = jnp.where(bottom, 0.0, pltpu.roll(flux_n, 1, 1))
                    stepped = (cell[h] - (flux_e[h] - flux_w[h])) - (flux_n - flux_s)
                    value[n][h] = (rhs[n][h] + coupling_below[h] * value[n][h]) * scale[h]
                    value_ref[n, k + 1, hs[h], :] = value[n][h]
                    rhs[n][h] = thick[h] * stepped
            thick_below, coupling_below = thick, coupling
        for h in range(halves):
            for n in range(count):
                rhs_ref[n, hs[h], :] = rhs[n][h]
            thickness_ref[hs[h], :] = thick_below[h]
            coupling_ref[hs[h], :] = coupling_below[h]

    @pl.when(step == blocks)
    def _():
        surface = gather_surface(count, cells, lat, received_ref)
        for h in range(halves):
            coupling = coupling_ref[hs[h], :]
            pivot = thickness_ref[hs[h], :] + coupling - coupling * gain_ref[1, hs[h], :]
            scale = 1.0 / pivot
            wet = limit_ref[2, hs[h], :] > 0.0
            for n in range(count):
                spot = n * cells + h * HALF
                rhs = rhs_ref[n, hs[h], :] + jnp.where(wet, surface[spot : spot + HALF], 0.0)
                value_ref[n, 0, hs[h], :] = (rhs + coupling * value_ref[n, 1, hs[h], :]) * scale
        gain_ref[0] = jnp.zeros((cells, lat), F32)
        rhs_ref[...] = jnp.zeros_like(rhs_ref)

    @pl.when(step >= blocks)
    def _():
        block = step - blocks
        solved = [[rhs_ref[n, s, :] for s in hs] for n in range(count)]
        for here in range(chunk):
            k = block * chunk + here
            for h in range(halves):
                gain = gain_ref[k, hs[h], :]
                for n in range(count):
                    solved[n][h] = value_ref[n, k, hs[h], :] + gain * solved[n][h]
                    out_ref[n, here, hs[h], :] = solved[n][h]
        for h in range(halves):
            for n in range(count):
                rhs_ref[n, hs[h], :] = solved[n][h]


def step_columns(
    tracer, east, north, kappa, mixing, thickness, depth, west, far, mirror, received
):
    count, levels, cells, lat = tracer.shape
    chunk = chunk_of(levels)
    blocks = levels // chunk
    whole = lambda x: pl.BlockSpec(x.shape, lambda s, nd=x.ndim: (0,) * nd)
    read = lambda s: jnp.maximum(blocks - 1 - s, 0)
    write = lambda s: jnp.maximum(s - blocks, 0)
    level = pl.BlockSpec((chunk, cells, lat), lambda s: (read(s), 0, 0))
    return pl.pallas_call(
        functools.partial(step_kernel, levels),
        grid=(2 * blocks,),
        out_shape=jax.ShapeDtypeStruct(tracer.shape, F32),
        in_specs=[pl.BlockSpec((count, chunk, cells, lat), lambda s: (0, read(s), 0, 0))]
        + [level] * 5
        + [whole(x) for x in (depth, west, far, mirror, received)],
        out_specs=pl.BlockSpec((count, chunk, cells, lat), lambda s: (0, write(s), 0, 0)),
        scratch_shapes=[
            pltpu.VMEM((count, levels + 1, cells, lat), F32),
            pltpu.VMEM((levels + 1, cells, lat), F32),
            pltpu.VMEM((count, cells, lat), F32),
            pltpu.VMEM((cells, lat), F32),
            pltpu.VMEM((cells, lat), F32),
            pltpu.VMEM((4, cells, lat), F32),
        ],
        compiler_params=pltpu.CompilerParams(vmem_limit_bytes=40 << 20),
        cost_estimate=pl.CostEstimate(flops=10**8, bytes_accessed=8 * 10**6, transcendentals=0),
        name="columns",
    )(tracer, east, north, kappa, mixing, thickness, depth, west, far, mirror, received)


def shards(
    tracer,
    east_speed,
    north_speed,
    diffusivity,
    mixing,
    thickness,
    depth_levels,
    air_flux,
    margin_tile,
    margin_source,
    margin_cell,
    margin_weight,
):
    tiles = lax.axis_size("lon")
    by_level = lambda x: jnp.transpose(x, (1, 0, 2))
    tracer = jnp.transpose(tracer, (0, 2, 1, 3))
    east, north, kappa = by_level(east_speed), by_level(north_speed), by_level(diffusivity)
    rows = lambda x: x.reshape(-1, LANES)
    up, down, mirror, messages = pack(
        tiles,
        tracer,
        east,
        north,
        kappa,
        depth_levels,
        air_flux,
        rows(margin_tile),
        rows(margin_source),
        rows(margin_cell),
        rows(margin_weight),
    )
    ring = [(i, (i + 1) % tiles) for i in range(tiles)]
    mirror = lax.ppermute(mirror, "lon", [(i, tiles - 1 - i) for i in range(tiles)])
    west = lax.ppermute(up, "lon", ring)
    far = lax.ppermute(down, "lon", [(j, i) for i, j in ring])
    received = lax.all_to_all(messages, "lon", split_axis=0, concat_axis=0, tiled=True)
    out = step_columns(
        tracer,
        east,
        north,
        kappa,
        by_level(mixing),
        by_level(thickness),
        depth_levels,
        west,
        far,
        mirror,
        received,
    )
    return jnp.transpose(out, (0, 2, 1, 3))


def solution(mesh):
    placed = (
        P(None, "lon", None, "ens"),
        P("lon", None, "ens"),
        P("lon", None, "ens"),
        P("lon", None, "ens"),
        P("lon", None, "ens"),
        P("lon", None, "ens"),
        P("lon", "ens"),
        P("ens", "lon"),
        P(("ens", "lon"), None),
        P(("ens", "lon")),
        P(("ens", "lon")),
        P(("ens", "lon")),
    )
    return jax.shard_map(
        shards, mesh=mesh, in_specs=placed, out_specs=P(None, "lon", None, "ens"), check_vma=False
    )
```

```python
import functools

import jax
import jax.numpy as jnp
from jax import lax
from jax.experimental import pallas as pl
from jax.experimental.pallas import tpu as pltpu
from jax.sharding import PartitionSpec as P

CAP = 64
HALF = 8
GROUP = 5
LANES = 128
F32 = jnp.float32


def chunk_of(levels):
    return max(c for c in range(GROUP, 4 * GROUP, GROUP) if levels % c == 0)


def thirds(x):
    high = x.astype(jnp.bfloat16)
    rest = x - high.astype(F32)
    mid = rest.astype(jnp.bfloat16)
    low = (rest - mid.astype(F32)).astype(jnp.bfloat16)
    return high, mid, low


def lane_ids(rows):
    return lax.broadcasted_iota(jnp.int32, (rows, LANES), 1)


def row_ids(rows):
    return lax.broadcasted_iota(jnp.int32, (rows, LANES), 0)


def dot_nt(a, b):
    return lax.dot_general(a, b, (((1,), (1,)), ((), ())), preferred_element_type=F32)


def dot_nn(a, b):
    return lax.dot_general(a, b, (((1,), (0,)), ((), ())), preferred_element_type=F32)


def make_messages(tiles, air_ref, tile_ref, source_ref, cell_ref, weight_ref, msg_ref):
    count, air_cells = air_ref.shape
    chunks = tile_ref.shape[0]
    one, zero = jnp.ones((), F32), jnp.zeros((), F32)
    rows = [slice(c, c + 1) for c in range(chunks)]
    owns = [
        jnp.broadcast_to(tile_ref[r, :], (tiles, LANES)) == row_ids(tiles) for r in rows
    ]
    owned = jnp.concatenate([jnp.where(o, one, zero) for o in owns], axis=0).astype(jnp.bfloat16)
    earlier = jnp.where(row_ids(LANES) < lane_ids(LANES), one, zero).astype(jnp.bfloat16)
    prior = dot_nn(owned, earlier)
    total = dot_nn(owned, jnp.ones((LANES, LANES), jnp.bfloat16))
    air_parts = jnp.concatenate(
        [p.astype(F32) for p in thirds(air_ref[...])], axis=0
    ).astype(jnp.bfloat16)
    carry = jnp.zeros((tiles, LANES), F32)
    slots, parts = [], []
    for c in range(chunks):
        span = slice(c * tiles, (c + 1) * tiles)
        slots.append(
            jnp.sum(jnp.where(owns[c], prior[span] + carry, zero), axis=0, keepdims=True)
        )
        carry = carry + total[span]
        picked = jnp.broadcast_to(source_ref[rows[c], :], (air_cells, LANES)) == row_ids(air_cells)
        taken = dot_nn(air_parts, jnp.where(picked, one, zero).astype(jnp.bfloat16))
        flux = taken[:count] + taken[count : 2 * count] + taken[2 * count : 3 * count]
        payload = weight_ref[rows[c], :] * flux
        record = jnp.concatenate(
            [
                payload,
                cell_ref[rows[c], :].astype(F32),
                jnp.zeros((HALF - count - 1, LANES), F32),
            ],
            axis=0,
        )
        parts.append([p.astype(F32) for p in thirds(record)])
    slot_hot = jnp.concatenate(
        [
            jnp.where(
                jnp.broadcast_to(s.astype(jnp.int32), (LANES, LANES)) == row_ids(LANES), one, zero
            ).astype(jnp.bfloat16)
            for s in slots
        ],
        axis=1,
    )
    out = jnp.zeros((tiles * HALF, LANES), F32)
    for part in range(3):
        spread = jnp.concatenate(
            [
                jnp.concatenate(
                    [
                        jnp.where(
                            jnp.broadcast_to(tile_ref[rows[c], :], (HALF, LANES)) == d,
                            parts[c][part],
                            zero,
                        )
                        for d in range(tiles)
                    ],
                    axis=0,
                ).astype(jnp.bfloat16)
                for c in range(chunks)
            ],
            axis=1,
        )
        out = out + dot_nt(spread, slot_hot)
    msg_ref[...] = out.reshape(tiles, HALF, LANES)


def pack_kernel(
    levels,
    tiles,
    tracer_hbm,
    east_hbm,
    north_hbm,
    kappa_hbm,
    depth_ref,
    air_ref,
    tile_ref,
    source_ref,
    cell_ref,
    weight_ref,
    up_ref,
    down_ref,
    mirror_ref,
    own_ref,
    msg_ref,
    tracer_ref,
    east_ref,
    north_ref,
    kappa_ref,
    sems,
):
    count, _, cells, _ = tracer_ref.shape
    fields = count + 2
    chunk = chunk_of(levels)
    blocks = levels // chunk
    lane = lane_ids(cells)

    def copies(block):
        span = pl.ds(block * chunk, chunk)
        pairs = [
            (tracer_hbm.at[:, span], tracer_ref.at[:, span]),
            (north_hbm.at[span], north_ref.at[span]),
            (kappa_hbm.at[span], kappa_ref.at[span]),
            (east_hbm.at[span, pl.ds(cells - HALF, HALF)], east_ref.at[span]),
        ]
        return [
            pltpu.make_async_copy(src, dst, sems.at[block, i]) for i, (src, dst) in enumerate(pairs)
        ]

    for block in range(blocks):
        for copy in copies(block):
            copy.start()

    depth = depth_ref[...].astype(F32)
    up_ref[fields * levels : fields * levels + 1, :] = depth[cells - 1 : cells]
    down_ref[(fields - 1) * levels : (fields - 1) * levels + 1, :] = depth[0:1]
    make_messages(tiles, air_ref, tile_ref, source_ref, cell_ref, weight_ref, msg_ref)

    def several(group, columns):
        columns = list(columns)
        for inner in range(GROUP):
            k = group * GROUP + inner
            slabs = [tracer_ref[n, k] for n in range(count)] + [north_ref[k], kappa_ref[k]]
            for f in range(fields):
                columns[f] = jnp.where(lane == k, pltpu.roll(slabs[f], k + 1, 1), columns[f])
                if f < count:
                    up_ref[pl.ds(f * levels + k, 1), :] = slabs[f][cells - 1 : cells]
                    down_ref[pl.ds(f * levels + k, 1), :] = slabs[f][0:1]
            up_ref[pl.ds(count * levels + k, 1), :] = east_ref[k][HALF - 1 : HALF]
            up_ref[pl.ds((count + 1) * levels + k, 1), :] = slabs[count + 1][cells - 1 : cells]
            down_ref[pl.ds(count * levels + k, 1), :] = slabs[count + 1][0:1]
        return tuple(columns)

    def whole_block(block, columns):
        for copy in copies(block):
            copy.wait()
        first = block * (chunk // GROUP)
        return lax.fori_loop(first, first + chunk // GROUP, several, columns)

    columns = [jnp.zeros((cells, LANES), F32)] * fields
    columns[0] = jnp.where(lane == levels, pltpu.roll(depth, levels + 1, 1), 0.0)
    columns = lax.fori_loop(0, blocks, whole_block, tuple(columns))
    for f in range(fields):
        own_ref[f * cells : (f + 1) * cells, :] = columns[f]
        for i in range(cells):
            spot = f * cells + cells - 1 - i
            mirror_ref[spot : spot + 1, :] = columns[f][i : i + 1]


def pack(tiles, tracer, east, north, kappa, depth, air, tile, source, cell, weight):
    count, levels, cells, lat = tracer.shape
    fields = count + 2
    out = [
        jax.ShapeDtypeStruct((-(-(fields * levels + 1) // HALF) * HALF, lat), F32),
        jax.ShapeDtypeStruct((-(-((fields - 1) * levels + 1) // HALF) * HALF, lat), F32),
        jax.ShapeDtypeStruct((fields * cells, LANES), F32),
        jax.ShapeDtypeStruct((fields * cells, LANES), F32),
        jax.ShapeDtypeStruct((tiles, HALF, LANES), F32),
    ]
    vmem = pl.BlockSpec(memory_space=pltpu.VMEM)
    return pl.pallas_call(
        functools.partial(pack_kernel, levels, tiles),
        out_shape=out,
        in_specs=[pl.BlockSpec(memory_space=pl.ANY)] * 4 + [vmem] * 6,
        out_specs=[vmem] * 5,
        scratch_shapes=[
            pltpu.VMEM(tracer.shape, F32),
            pltpu.VMEM((levels, HALF, lat), F32),
            pltpu.VMEM(north.shape, F32),
            pltpu.VMEM(kappa.shape, F32),
            pltpu.SemaphoreType.DMA((levels // chunk_of(levels), 4)),
        ],
        compiler_params=pltpu.CompilerParams(vmem_limit_bytes=62 << 20),
        cost_estimate=pl.CostEstimate(flops=10**7, bytes_accessed=4 * 10**6, transcendentals=0),
        name="pack",
    )(tracer, east, north, kappa, depth, air, tile, source, cell, weight)


def gather_surface(count, cells, lat, received_ref):
    tiles = received_ref.shape[0]
    shift = lat.bit_length() - 1
    values, spots = [[], [], []], []
    one, zero = jnp.ones((), F32), jnp.zeros((), F32)
    left, right = [[], [], []], []
    for t in range(tiles):
        block = received_ref[t]
        cell = block[count : count + 1].astype(jnp.int32)
        row = jnp.broadcast_to(lax.shift_right_logical(cell, shift), (cells, LANES))
        col = jnp.broadcast_to(cell & (lat - 1), (lat, LANES))
        right.append(jnp.where(col == row_ids(lat), one, zero).astype(jnp.bfloat16))
        hit = row == row_ids(cells)
        for p, part in enumerate(thirds(block)):
            part = part.astype(F32)
            left[p].append(
                jnp.concatenate(
                    [
                        jnp.where(hit, jnp.broadcast_to(part[n : n + 1], (cells, LANES)), zero)
                        for n in range(count)
                    ],
                    axis=0,
                ).astype(jnp.bfloat16)
            )
    spread = jnp.concatenate(right, axis=1)
    return sum(dot_nt(jnp.concatenate(left[p], axis=1), spread) for p in range(3))


def step_kernel(
    levels,
    tracer_hbm,
    east_hbm,
    north_hbm,
    kappa_hbm,
    mixing_hbm,
    thick_hbm,
    depth_hbm,
    west_hbm,
    far_hbm,
    own_hbm,
    mirror_hbm,
    received_hbm,
    out_hbm,
    tracer_ref,
    east_ref,
    north_ref,
    kappa_ref,
    mixing_ref,
    thick_ref,
    depth_ref,
    west_ref,
    far_ref,
    own_ref,
    mirror_ref,
    received_ref,
    value_ref,
    gain_ref,
    limit_ref,
    fold_ref,
    small_sems,
    sems,
    out_sems,
):
    count, _, cells, lat = tracer_ref.shape
    chunk = chunk_of(levels)
    blocks = levels // chunk

    def copies(block):
        span = pl.ds(block * chunk, chunk)
        pairs = [(tracer_hbm.at[:, span], tracer_ref.at[:, span])] + [
            (hbm.at[span], ref.at[span])
            for hbm, ref in (
                (kappa_hbm, kappa_ref),
                (east_hbm, east_ref),
                (north_hbm, north_ref),
                (thick_hbm, thick_ref),
                (mixing_hbm, mixing_ref),
            )
        ]
        return [
            pltpu.make_async_copy(src, dst, sems.at[block, i]) for i, (src, dst) in enumerate(pairs)
        ]

    def result(block):
        span = pl.ds(block * chunk, chunk)
        return pltpu.make_async_copy(
            value_ref.at[:, span], out_hbm.at[:, span], out_sems.at[block]
        )

    small = [
        pltpu.make_async_copy(src, dst, small_sems.at[i])
        for i, (src, dst) in enumerate(
            (
                (own_hbm, own_ref),
                (mirror_hbm, mirror_ref),
                (depth_hbm, depth_ref),
                (far_hbm, far_ref),
                (west_hbm, west_ref),
                (received_hbm, received_ref),
            )
        )
    ]
    for copy in small[:-1]:
        copy.start()
    for block in range(blocks - 1, -1, -1):
        for copy in copies(block):
            copy.start()
    small[-1].start()
    halves = cells // HALF
    fields = count + 2
    row8 = row_ids(HALF)
    lane8 = lane_ids(HALF)
    top = lane8 == lat - 1
    bottom = lane8 == 0
    first = row8 == 0
    last = row8 == HALF - 1
    hs = [slice(h * HALF, (h + 1) * HALF) for h in range(halves)]

    def from_east(parts, halo):
        turned = [pltpu.roll(p, HALF - 1, 0) for p in parts]
        return [
            jnp.where(last, turned[h + 1] if h + 1 < halves else halo, turned[h])
            for h in range(halves)
        ]

    def from_west(parts, halo):
        turned = [pltpu.roll(p, 1, 0) for p in parts]
        return [
            jnp.where(first, turned[h - 1] if h > 0 else halo, turned[h]) for h in range(halves)
        ]

    def row_of(ref, index):
        return jnp.broadcast_to(ref[pl.ds(index, 1), :], (HALF, lat))

    for copy in small[:2]:
        copy.wait()
    for h in range(halves):
        mine, other = [
            [ref[f * cells + h * HALF : f * cells + (h + 1) * HALF, :] for f in range(fields)]
            for ref in (own_ref, mirror_ref)
        ]
        mean = 0.5 * (mine[count + 1] + other[count + 1])
        speed = 0.5 * (mine[count] - other[count])
        deep = jnp.minimum(mine[0], other[0])
        deep = jnp.broadcast_to(deep[:, levels : levels + 1], (HALF, LANES))
        open_face = deep > lane8.astype(F32)
        near = jnp.where(open_face, jnp.maximum(speed, 0.0) + mean, 0.0)
        far = jnp.where(open_face, jnp.minimum(speed, 0.0) - mean, 0.0)
        for n in range(count):
            flux = near * mine[n] + far * other[n]
            for k in range(levels):
                fold_ref[k, n, hs[h], :] = pltpu.roll(flux, lat - 1 - k, 1)
    for copy in small[2:-1]:
        copy.wait()
    depth = [depth_ref[s, :].astype(F32) for s in hs]
    depth_east = from_east(depth, row_of(far_ref, (fields - 1) * levels))
    limit_here = depth
    limit_east = [jnp.minimum(depth[h], depth_east[h]) for h in range(halves)]
    limit_north = [
        jnp.where(top, 0.0, jnp.minimum(depth[h], pltpu.roll(depth[h], lat - 1, 1)))
        for h in range(halves)
    ]
    limit_west = jnp.minimum(
        jnp.broadcast_to(depth[0][0:1], (HALF, lat)), row_of(west_ref, fields * levels)
    )

    def several(group, state):
        rhs, thick_below, coupling_below, value, gain = jax.tree.map(lambda x: x, state)
        for inner in range(GROUP):
            k = levels - 1 - (group * GROUP + inner)
            level = k.astype(F32)
            kappa = [kappa_ref[k, s, :] for s in hs]
            speed = [east_ref[k, s, :] for s in hs]
            kappa_east = from_east(kappa, row_of(far_ref, count * levels + k))
            near_e, far_e = [], []
            for h in range(halves):
                mean = 0.5 * (kappa[h] + kappa_east[h])
                open_face = limit_east[h] > level
                near_e.append(jnp.where(open_face, jnp.maximum(speed[h], 0.0) + mean, 0.0))
                far_e.append(jnp.where(open_face, jnp.minimum(speed[h], 0.0) - mean, 0.0))
            speed_w = row_of(west_ref, count * levels + k)
            kappa_w = row_of(west_ref, (count + 1) * levels + k)
            mean = 0.5 * (kappa_w + jnp.broadcast_to(kappa[0][0:1], (HALF, lat)))
            open_face = limit_west > level
            near_w = jnp.where(open_face, jnp.maximum(speed_w, 0.0) + mean, 0.0)
            far_w = jnp.where(open_face, jnp.minimum(speed_w, 0.0) - mean, 0.0)
            near_n, far_n = [], []
            for h in range(halves):
                speed_n = north_ref[k, hs[h], :]
                mean = 0.5 * (kappa[h] + pltpu.roll(kappa[h], lat - 1, 1))
                open_face = limit_north[h] > level
                near_n.append(jnp.where(open_face, jnp.maximum(speed_n, 0.0) + mean, 0.0))
                far_n.append(jnp.where(open_face, jnp.minimum(speed_n, 0.0) - mean, 0.0))
            thick = [thick_ref[k, s, :] for s in hs]
            coupling, scale = [], []
            for h in range(halves):
                here = 2.0 * mixing_ref[k, hs[h], :] / (thick[h] + thick_below[h])
                here = jnp.where(limit_here[h] > level + 1.0, here, 0.0)
                coupling.append(here)
                pivot = thick_below[h] + here + coupling_below[h] - coupling_below[h] * gain[h]
                scale.append(1.0 / pivot)
                gain[h] = here * scale[h]
                gain_ref[k + 1, hs[h], :] = gain[h]
            for n in range(count):
                cell = [tracer_ref[n, k, s, :] for s in hs]
                cell_east = from_east(cell, row_of(far_ref, n * levels + k))
                flux_e = [near_e[h] * cell[h] + far_e[h] * cell_east[h] for h in range(halves)]
                flux_in = near_w * row_of(west_ref, n * levels + k) + far_w * jnp.broadcast_to(
                    cell[0][0:1], (HALF, lat)
                )
                flux_w = from_west(flux_e, flux_in)
                for h in range(halves):
                    flux_n = near_n[h] * cell[h] + far_n[h] * pltpu.roll(cell[h], lat - 1, 1)
                    flux_n = jnp.where(top, fold_ref[k, n, hs[h], :], flux_n)
                    flux_s = jnp.where(bottom, 0.0, pltpu.roll(flux_n, 1, 1))
                    stepped = (cell[h] - (flux_e[h] - flux_w[h])) - (flux_n - flux_s)
                    value[n][h] = (rhs[n][h] + coupling_below[h] * value[n][h]) * scale[h]
                    value_ref[n, k + 1, hs[h], :] = value[n][h]
                    rhs[n][h] = thick[h] * stepped
            thick_below, coupling_below = thick, coupling
        return rhs, thick_below, coupling_below, value, gain

    def eliminate(turn, state):
        for copy in copies(blocks - 1 - turn):
            copy.wait()
        first = turn * (chunk // GROUP)
        return lax.fori_loop(first, first + chunk // GROUP, several, state)

    zero = [jnp.zeros((HALF, lat), F32)] * halves
    state = ([zero] * count, [jnp.ones((HALF, lat), F32)] * halves, zero, [zero] * count, zero)
    rhs, thick, coupling, value, gain = lax.fori_loop(0, blocks, eliminate, state)
    small[-1].wait()
    surface = gather_surface(count, cells, lat, received_ref)
    solved = []
    for n in range(count):
        solved.append([])
        for h in range(halves):
            scale = 1.0 / (thick[h] + coupling[h] - coupling[h] * gain[h])
            spot = n * cells + h * HALF
            flux = jnp.where(limit_here[h] > 0.0, surface[spot : spot + HALF], 0.0)
            solved[n].append((rhs[n][h] + flux + coupling[h] * value[n][h]) * scale)
            value_ref[n, 0, hs[h], :] = solved[n][h]

    def descend(group, solved):
        solved = jax.tree.map(lambda x: x, solved)
        for inner in range(GROUP):
            k = group * GROUP + inner
            for h in range(halves):
                gain = gain_ref[k, hs[h], :]
                for n in range(count):
                    solved[n][h] = value_ref[n, k, hs[h], :] + gain * solved[n][h]
                    value_ref[n, k, hs[h], :] = solved[n][h]
        return solved

    def substitute(block, solved):
        first = block * (chunk // GROUP)
        solved = lax.fori_loop(first, first + chunk // GROUP, descend, solved)
        result(block).start()
        return solved

    gain_ref[0] = jnp.zeros((cells, lat), F32)
    lax.fori_loop(0, blocks, substitute, solved)
    for block in range(blocks):
        result(block).wait()


def step_columns(
    tracer, east, north, kappa, mixing, thickness, depth, west, far, own, mirror, received
):
    count, levels, cells, lat = tracer.shape
    blocks = levels // chunk_of(levels)
    operands = [tracer, east, north, kappa, mixing, thickness]
    operands += [depth, west, far, own, mirror, received]
    return pl.pallas_call(
        functools.partial(step_kernel, levels),
        out_shape=jax.ShapeDtypeStruct(tracer.shape, F32),
        in_specs=[pl.BlockSpec(memory_space=pl.ANY)] * len(operands),
        out_specs=pl.BlockSpec(memory_space=pl.ANY),
        scratch_shapes=[pltpu.VMEM(x.shape, x.dtype) for x in operands]
        + [
            pltpu.VMEM((count, levels + 1, cells, lat), F32),
            pltpu.VMEM((levels + 1, cells, lat), F32),
            pltpu.VMEM((4, cells, lat), F32),
            pltpu.VMEM((levels, count, cells, lat), F32),
            pltpu.SemaphoreType.DMA((6,)),
            pltpu.SemaphoreType.DMA((blocks, 6)),
            pltpu.SemaphoreType.DMA((blocks,)),
        ],
        compiler_params=pltpu.CompilerParams(vmem_limit_bytes=62 << 20),
        cost_estimate=pl.CostEstimate(flops=10**8, bytes_accessed=8 * 10**6, transcendentals=0),
        name="columns",
    )(*operands)


def shards(
    tracer,
    east_speed,
    north_speed,
    diffusivity,
    mixing,
    thickness,
    depth_levels,
    air_flux,
    margin_tile,
    margin_source,
    margin_cell,
    margin_weight,
):
    tiles = lax.axis_size("lon")
    by_level = lambda x: jnp.transpose(x, (1, 0, 2))
    tracer = jnp.transpose(tracer, (0, 2, 1, 3))
    east, north, kappa = by_level(east_speed), by_level(north_speed), by_level(diffusivity)
    rows = lambda x: x.reshape(-1, LANES)
    up, down, mirror, own, messages = pack(
        tiles,
        tracer,
        east,
        north,
        kappa,
        depth_levels,
        air_flux,
        rows(margin_tile),
        rows(margin_source),
        rows(margin_cell),
        rows(margin_weight),
    )
    ring = [(i, (i + 1) % tiles) for i in range(tiles)]
    mirror = lax.ppermute(mirror, "lon", [(i, tiles - 1 - i) for i in range(tiles)])
    west = lax.ppermute(up, "lon", ring)
    far = lax.ppermute(down, "lon", [(j, i) for i, j in ring])
    received = lax.all_to_all(messages, "lon", split_axis=0, concat_axis=0, tiled=True)
    out = step_columns(
        tracer,
        east,
        north,
        kappa,
        by_level(mixing),
        by_level(thickness),
        depth_levels,
        west,
        far,
        own,
        mirror,
        received,
    )
    return jnp.transpose(out, (0, 2, 1, 3))


def solution(mesh):
    placed = (
        P(None, "lon", None, "ens"),
        P("lon", None, "ens"),
        P("lon", None, "ens"),
        P("lon", None, "ens"),
        P("lon", None, "ens"),
        P("lon", None, "ens"),
        P("lon", "ens"),
        P("ens", "lon"),
        P(("ens", "lon"), None),
        P(("ens", "lon")),
        P(("ens", "lon")),
        P(("ens", "lon")),
    )
    return jax.shard_map(
        shards, mesh=mesh, in_specs=placed, out_specs=P(None, "lon", None, "ens"), check_vma=False
    )
```

```python
import functools

import jax
import jax.numpy as jnp
from jax import lax
from jax.experimental import pallas as pl
from jax.experimental.pallas import tpu as pltpu
from jax.sharding import PartitionSpec as P

CAP = 64
HALF = 8
GROUP = 5
AHEAD = 2
PACK_AHEAD = 4
LANES = 128
F32 = jnp.float32


def chunk_of(levels):
    return max(c for c in range(GROUP, 4 * GROUP, GROUP) if levels % c == 0)


def thirds(x):
    high = x.astype(jnp.bfloat16)
    rest = x - high.astype(F32)
    mid = rest.astype(jnp.bfloat16)
    low = (rest - mid.astype(F32)).astype(jnp.bfloat16)
    return high, mid, low


VMEM = pl.BlockSpec(memory_space=pltpu.VMEM)
ANY = pl.BlockSpec(memory_space=pl.ANY)


def in_hbm(*arrays):
    return [pltpu.with_memory_space_constraint(x, pltpu.HBM) for x in arrays]


def in_vmem(*arrays):
    return [pltpu.with_memory_space_constraint(x, pltpu.VMEM) for x in arrays]


def lane_ids(rows):
    return lax.broadcasted_iota(jnp.int32, (rows, LANES), 1)


def row_ids(rows):
    return lax.broadcasted_iota(jnp.int32, (rows, LANES), 0)


def dot_nt(a, b):
    return lax.dot_general(a, b, (((1,), (1,)), ((), ())), preferred_element_type=F32)


def dot_nn(a, b):
    return lax.dot_general(a, b, (((1,), (0,)), ((), ())), preferred_element_type=F32)


def make_messages(tiles, air_ref, tile_ref, source_ref, cell_ref, weight_ref, msg_ref):
    count, air_cells = air_ref.shape
    chunks = tile_ref.shape[0]
    one, zero = jnp.ones((), F32), jnp.zeros((), F32)
    rows = [slice(c, c + 1) for c in range(chunks)]
    owns = [
        jnp.broadcast_to(tile_ref[r, :], (tiles, LANES)) == row_ids(tiles) for r in rows
    ]
    owned = jnp.concatenate([jnp.where(o, one, zero) for o in owns], axis=0).astype(jnp.bfloat16)
    earlier = jnp.where(row_ids(LANES) < lane_ids(LANES), one, zero).astype(jnp.bfloat16)
    prior = dot_nn(owned, earlier)
    total = dot_nn(owned, jnp.ones((LANES, LANES), jnp.bfloat16))
    air_parts = jnp.concatenate(
        [p.astype(F32) for p in thirds(air_ref[...])], axis=0
    ).astype(jnp.bfloat16)
    carry = jnp.zeros((tiles, LANES), F32)
    slots, parts = [], []
    for c in range(chunks):
        span = slice(c * tiles, (c + 1) * tiles)
        slots.append(
            jnp.sum(jnp.where(owns[c], prior[span] + carry, zero), axis=0, keepdims=True)
        )
        carry = carry + total[span]
        picked = jnp.broadcast_to(source_ref[rows[c], :], (air_cells, LANES)) == row_ids(air_cells)
        taken = dot_nn(air_parts, jnp.where(picked, one, zero).astype(jnp.bfloat16))
        flux = taken[:count] + taken[count : 2 * count] + taken[2 * count : 3 * count]
        payload = weight_ref[rows[c], :] * flux
        record = jnp.concatenate(
            [
                payload,
                cell_ref[rows[c], :].astype(F32),
                jnp.zeros((HALF - count - 1, LANES), F32),
            ],
            axis=0,
        )
        parts.append([p.astype(F32) for p in thirds(record)])
    slot_hot = jnp.concatenate(
        [
            jnp.where(
                jnp.broadcast_to(s.astype(jnp.int32), (LANES, LANES)) == row_ids(LANES), one, zero
            ).astype(jnp.bfloat16)
            for s in slots
        ],
        axis=1,
    )
    out = jnp.zeros((tiles * HALF, LANES), F32)
    for part in range(3):
        spread = jnp.concatenate(
            [
                jnp.concatenate(
                    [
                        jnp.where(
                            jnp.broadcast_to(tile_ref[rows[c], :], (HALF, LANES)) == d,
                            parts[c][part],
                            zero,
                        )
                        for d in range(tiles)
                    ],
                    axis=0,
                ).astype(jnp.bfloat16)
                for c in range(chunks)
            ],
            axis=1,
        )
        out = out + dot_nt(spread, slot_hot)
    cells = pltpu.roll(pltpu.roll(out, CAP, 1).reshape(tiles, HALF, LANES), HALF - count, 1)
    out = out.reshape(tiles, HALF, LANES)
    head = lax.broadcasted_iota(jnp.int32, out.shape, 1) == 0
    msg_ref[...] = jnp.where(head, out + cells, out)[:, :count]


def pack_kernel(
    levels,
    tiles,
    tracer_hbm,
    east_hbm,
    north_hbm,
    kappa_hbm,
    depth_hbm,
    air_hbm,
    tile_hbm,
    source_hbm,
    cell_hbm,
    weight_hbm,
    up_ref,
    down_ref,
    mirror_ref,
    msg_ref,
    own_ref,
    tracer_ref,
    east_ref,
    north_ref,
    kappa_ref,
    depth_ref,
    air_ref,
    tile_ref,
    source_ref,
    cell_ref,
    weight_ref,
    sems,
    small_sems,
):
    count, _, cells, _ = tracer_ref.shape
    fields = count + 2
    chunk = chunk_of(levels)
    blocks = levels // chunk
    lane = lane_ids(cells)

    def copies(block):
        span = pl.ds(block * chunk, chunk)
        pairs = [
            (tracer_hbm.at[:, span], tracer_ref.at[:, span]),
            (north_hbm.at[span], north_ref.at[span]),
            (kappa_hbm.at[span], kappa_ref.at[span]),
            (east_hbm.at[span, pl.ds(cells - HALF, HALF)], east_ref.at[span]),
        ]
        return [
            pltpu.make_async_copy(src, dst, sems.at[block, i]) for i, (src, dst) in enumerate(pairs)
        ]

    small = [
        pltpu.make_async_copy(src, dst, small_sems.at[i])
        for i, (src, dst) in enumerate(
            (
                (tile_hbm, tile_ref),
                (air_hbm, air_ref),
                (source_hbm, source_ref),
                (cell_hbm, cell_ref),
                (weight_hbm, weight_ref),
                (depth_hbm, depth_ref),
            )
        )
    ]
    for copy in small:
        copy.start()
    for block in range(PACK_AHEAD):
        for copy in copies(block):
            copy.start()
    for copy in small:
        copy.wait()

    depth = depth_ref[...].astype(F32)
    up_ref[fields * levels : fields * levels + 1, :] = depth[cells - 1 : cells]
    down_ref[(fields - 1) * levels : (fields - 1) * levels + 1, :] = depth[0:1]
    make_messages(tiles, air_ref, tile_ref, source_ref, cell_ref, weight_ref, msg_ref)

    def several(group, columns):
        columns = list(columns)
        for inner in range(chunk):
            k = group * chunk + inner
            slabs = [tracer_ref[n, k] for n in range(count)] + [north_ref[k], kappa_ref[k]]
            for f in range(fields):
                columns[f] = jnp.where(lane == k, pltpu.roll(slabs[f], k + 1, 1), columns[f])
                if f < count:
                    up_ref[pl.ds(f * levels + k, 1), :] = slabs[f][cells - 1 : cells]
                    down_ref[pl.ds(f * levels + k, 1), :] = slabs[f][0:1]
            up_ref[pl.ds(count * levels + k, 1), :] = east_ref[k, HALF - 1 : HALF, :]
            up_ref[pl.ds((count + 1) * levels + k, 1), :] = slabs[count + 1][cells - 1 : cells]
            down_ref[pl.ds(count * levels + k, 1), :] = slabs[count + 1][0:1]
        return tuple(columns)

    def whole_block(block, columns):
        for copy in copies(block):
            copy.wait()

        @pl.when(block + PACK_AHEAD < blocks)
        def _():
            for copy in copies(block + PACK_AHEAD):
                copy.start()

        return several(block, columns)

    columns = [jnp.zeros((cells, LANES), F32)] * fields
    columns = lax.fori_loop(0, blocks, whole_block, tuple(columns))
    last = depth.shape[1] - 1
    columns = [*columns, jnp.broadcast_to(depth[:, last : last + 1], (cells, LANES))]
    for f in range(fields + 1):
        own_ref[f * cells : (f + 1) * cells, :] = columns[f]
        for i in range(cells):
            spot = f * cells + cells - 1 - i
            mirror_ref[spot : spot + 1, :] = columns[f][i : i + 1]


def pack(tiles, fields, small):
    count, levels, cells, lat = fields[0].shape
    rows = lambda n: jax.ShapeDtypeStruct((-(-n // HALF) * HALF, lat), F32)
    return pl.pallas_call(
        functools.partial(pack_kernel, levels, tiles),
        out_shape=[
            rows((count + 2) * levels + 1),
            rows((count + 1) * levels + 1),
            jax.ShapeDtypeStruct(((count + 3) * cells, LANES), F32),
            jax.ShapeDtypeStruct((tiles, count, LANES), F32),
            pltpu.HBM(((count + 3) * cells, LANES), F32),
        ],
        in_specs=[ANY] * (len(fields) + len(small)),
        out_specs=[VMEM] * 5,
        scratch_shapes=[
            pltpu.VMEM((count, levels, cells, lat), F32),
            pltpu.VMEM((levels, HALF, lat), F32),
            pltpu.VMEM((levels, cells, lat), F32),
            pltpu.VMEM((levels, cells, lat), F32),
        ]
        + [pltpu.VMEM(x.shape, x.dtype) for x in small]
        + [
            pltpu.SemaphoreType.DMA((levels // chunk_of(levels), 4)),
            pltpu.SemaphoreType.DMA((6,)),
        ],
        compiler_params=pltpu.CompilerParams(vmem_limit_bytes=12 << 20),
        cost_estimate=pl.CostEstimate(flops=10**7, bytes_accessed=4 * 10**6, transcendentals=0),
        name="pack",
    )(*in_hbm(*fields, *small))


def gather_surface(count, cells, lat, received_ref):
    tiles = received_ref.shape[0]
    shift = lat.bit_length() - 1
    one, zero = jnp.ones((), F32), jnp.zeros((), F32)
    left, right = [[], [], []], []
    early = lane_ids(count) < CAP
    for t in range(0, tiles, 2):
        even, odd = received_ref[t], received_ref[t + 1]
        block = jnp.where(early, even, pltpu.roll(odd, CAP, 1))
        cell = jnp.where(early, pltpu.roll(even, CAP, 1), odd)[0:1].astype(jnp.int32)
        row = jnp.broadcast_to(lax.shift_right_logical(cell, shift), (cells, LANES))
        col = jnp.broadcast_to(cell & (lat - 1), (lat, LANES))
        right.append(jnp.where(col == row_ids(lat), one, zero).astype(jnp.bfloat16))
        hit = row == row_ids(cells)
        for p, part in enumerate(thirds(block)):
            part = part.astype(F32)
            left[p].append(
                jnp.concatenate(
                    [
                        jnp.where(hit, jnp.broadcast_to(part[n : n + 1], (cells, LANES)), zero)
                        for n in range(count)
                    ],
                    axis=0,
                ).astype(jnp.bfloat16)
            )
    spread = jnp.concatenate(right, axis=1)
    return sum(dot_nt(jnp.concatenate(left[p], axis=1), spread) for p in range(3))


def eliminate_kernel(
    levels,
    west_ref,
    far_ref,
    own_hbm,
    mirror_hbm,
    depth_hbm,
    tracer_hbm,
    kappa_hbm,
    north_hbm,
    east_hbm,
    thick_hbm,
    mixing_hbm,
    state_ref,
    own_ref,
    mirror_ref,
    depth_ref,
    tracer_ref,
    kappa_ref,
    north_ref,
    east_ref,
    thick_ref,
    mixing_ref,
    fold_ref,
    next_ref,
    part_ref,
    south_ref,
    small_sems,
    sems,
):
    count, _, cells, lat = tracer_ref.shape
    chunk = chunk_of(levels)
    blocks, groups = levels // chunk, chunk // GROUP

    def copies(block):
        span = pl.ds(block * chunk, chunk)
        pairs = [(tracer_hbm.at[:, span], tracer_ref.at[:, span])] + [
            (hbm.at[span], ref.at[span])
            for hbm, ref in (
                (kappa_hbm, kappa_ref),
                (north_hbm, north_ref),
                (east_hbm, east_ref),
                (thick_hbm, thick_ref),
                (mixing_hbm, mixing_ref),
            )
        ]
        return [
            pltpu.make_async_copy(src, dst, sems.at[block, i]) for i, (src, dst) in enumerate(pairs)
        ]

    def fetched(block):
        for copy in copies(block):
            copy.wait()

        @pl.when(block >= AHEAD)
        def _():
            for copy in copies(block - AHEAD):
                copy.start()

    small = [
        pltpu.make_async_copy(src, dst, small_sems.at[i])
        for i, (src, dst) in enumerate(
            ((own_hbm, own_ref), (mirror_hbm, mirror_ref), (depth_hbm, depth_ref))
        )
    ]
    for copy in small:
        copy.start()
    for block in range(blocks - 1, blocks - 1 - AHEAD, -1):
        for copy in copies(block):
            copy.start()
    halves = cells // HALF
    fields = count + 2
    row8 = row_ids(HALF)
    lane8 = lane_ids(HALF)
    top = lane8 == lat - 1
    bottom = lane8 == 0
    first = row8 == 0
    last = row8 == HALF - 1
    hs = [slice(h * HALF, (h + 1) * HALF) for h in range(halves)]

    def from_east(parts, halo):
        turned = [pltpu.roll(p, HALF - 1, 0) for p in parts]
        return [
            jnp.where(last, turned[h + 1] if h + 1 < halves else halo, turned[h])
            for h in range(halves)
        ]

    def from_west(parts, halo):
        turned = [pltpu.roll(p, 1, 0) for p in parts]
        return [
            jnp.where(first, turned[h - 1] if h > 0 else halo, turned[h]) for h in range(halves)
        ]

    def row_of(ref, index):
        return jnp.broadcast_to(ref[pl.ds(index, 1), :], (HALF, lat))

    for copy in small:
        copy.wait()
    for h in range(halves):
        mine, other = [
            [ref[f * cells + h * HALF : f * cells + (h + 1) * HALF, :] for f in range(fields + 1)]
            for ref in (own_ref, mirror_ref)
        ]
        mean = 0.5 * (mine[count + 1] + other[count + 1])
        speed = 0.5 * (mine[count] - other[count])
        open_face = jnp.minimum(mine[fields], other[fields]) > lane8.astype(F32)
        near = jnp.where(open_face, jnp.maximum(speed, 0.0) + mean, 0.0)
        far = jnp.where(open_face, jnp.minimum(speed, 0.0) - mean, 0.0)
        for n in range(count):
            flux = near * mine[n] + far * other[n]
            for k in range(levels):
                fold_ref[k, n, hs[h], :] = pltpu.roll(flux, lat - 1 - k, 1)
    depth = [depth_ref[s, :].astype(F32) for s in hs]
    depth_east = from_east(depth, row_of(far_ref, (fields - 1) * levels))
    limit_here = depth
    limit_east = [jnp.minimum(depth[h], depth_east[h]) for h in range(halves)]
    limit_north = [
        jnp.where(top, 0.0, jnp.minimum(depth[h], pltpu.roll(depth[h], lat - 1, 1)))
        for h in range(halves)
    ]
    limit_west = jnp.minimum(
        jnp.broadcast_to(depth[0][0:1], (HALF, lat)), row_of(west_ref, fields * levels)
    )

    def turned(group):
        for inner in range(GROUP):
            k = (levels - GROUP - group * GROUP) + (GROUP - 1 - inner)
            for s in hs:
                next_ref[inner, count, s, :] = pltpu.roll(kappa_ref[k, s, :], lat - 1, 1)
                for n in range(count):
                    next_ref[inner, n, s, :] = pltpu.roll(tracer_ref[n, k, s, :], lat - 1, 1)

    def fluxes(group):
        for inner in range(GROUP):
            k = (levels - GROUP - group * GROUP) + (GROUP - 1 - inner)
            level = k.astype(F32)
            kappa = [kappa_ref[k, s, :] for s in hs]
            speed = [east_ref[k, s, :] for s in hs]
            kappa_east = from_east(kappa, row_of(far_ref, count * levels + k))
            near_e, far_e = [], []
            for h in range(halves):
                mean = 0.5 * (kappa[h] + kappa_east[h])
                open_face = limit_east[h] > level
                near_e.append(jnp.where(open_face, jnp.maximum(speed[h], 0.0) + mean, 0.0))
                far_e.append(jnp.where(open_face, jnp.minimum(speed[h], 0.0) - mean, 0.0))
            speed_w = row_of(west_ref, count * levels + k)
            kappa_w = row_of(west_ref, (count + 1) * levels + k)
            mean = 0.5 * (kappa_w + jnp.broadcast_to(kappa[0][0:1], (HALF, lat)))
            open_face = limit_west > level
            near_w = jnp.where(open_face, jnp.maximum(speed_w, 0.0) + mean, 0.0)
            far_w = jnp.where(open_face, jnp.minimum(speed_w, 0.0) - mean, 0.0)
            near_n, far_n = [], []
            for h in range(halves):
                speed_n = north_ref[k, hs[h], :]
                mean = 0.5 * (kappa[h] + next_ref[inner, count, hs[h], :])
                open_face = limit_north[h] > level
                near_n.append(jnp.where(open_face, jnp.maximum(speed_n, 0.0) + mean, 0.0))
                far_n.append(jnp.where(open_face, jnp.minimum(speed_n, 0.0) - mean, 0.0))
            for n in range(count):
                cell = [tracer_ref[n, k, s, :] for s in hs]
                cell_east = from_east(cell, row_of(far_ref, n * levels + k))
                flux_e = [near_e[h] * cell[h] + far_e[h] * cell_east[h] for h in range(halves)]
                flux_in = near_w * row_of(west_ref, n * levels + k) + far_w * jnp.broadcast_to(
                    cell[0][0:1], (HALF, lat)
                )
                flux_w = from_west(flux_e, flux_in)
                for h in range(halves):
                    flux_n = near_n[h] * cell[h] + far_n[h] * next_ref[inner, n, hs[h], :]
                    flux_n = jnp.where(top, fold_ref[k, n, hs[h], :], flux_n)
                    part_ref[inner, n, hs[h], :] = (cell[h] - (flux_e[h] - flux_w[h])) - flux_n
                    south_ref[inner, n, hs[h], :] = pltpu.roll(flux_n, 1, 1)

    def solve(group, state):
        thick, coupling, value, gain, scale = jax.tree.map(lambda x: x, state)
        for inner in range(GROUP):
            k = (levels - GROUP - group * GROUP) + (GROUP - 1 - inner)
            above = jnp.maximum(k - 1, 0)
            closed = jnp.where(k > 0, k.astype(F32), float(levels))
            for h in range(halves):
                thick_above = thick_ref[above, hs[h], :]
                here = 2.0 * mixing_ref[above, hs[h], :] / (thick_above + thick[h])
                here = jnp.where(limit_here[h] > closed, here, 0.0)
                scale[h] = 1.0 / (thick[h] + here + coupling[h] - coupling[h] * gain[h])
                gain[h] = here * scale[h]
                state_ref[count * levels + k, hs[h], :] = gain[h]
                for n in range(count):
                    stepped = part_ref[inner, n, hs[h], :] + jnp.where(
                        bottom, 0.0, south_ref[inner, n, hs[h], :]
                    )
                    value[n][h] = (thick[h] * stepped + coupling[h] * value[n][h]) * scale[h]
                    state_ref[n * levels + k, hs[h], :] = value[n][h]
                thick[h], coupling[h] = thick_above, here
        return thick, coupling, value, gain, scale

    def turn(group, state):
        ahead = group + 1

        @pl.when(lax.rem(ahead, groups) == 0)
        def _():
            fetched(blocks - 1 - lax.div(ahead, groups))

        state = solve(group - 1, state)
        fluxes(group)
        turned(ahead)
        return state

    zero = [jnp.zeros((HALF, lat), F32)] * halves
    total = blocks * groups
    fetched(jnp.int32(blocks - 1))
    turned(jnp.int32(0))
    fluxes(jnp.int32(0))
    turned(jnp.int32(1))
    state = ([thick_ref[levels - 1, s, :] for s in hs], zero, [zero] * count, zero, zero)
    state = lax.fori_loop(1, total - 1, turn, state)
    state = solve(jnp.int32(total - 2), state)
    fluxes(jnp.int32(total - 1))
    scale = solve(jnp.int32(total - 1), state)[4]
    for h in range(halves):
        state_ref[count * levels, hs[h], :] = jnp.where(limit_here[h] > 0.0, scale[h], 0.0)


def substitute_kernel(state_ref, received_ref, out_hbm, out_ref, sems):
    count, levels, cells, lat = out_ref.shape
    chunk = chunk_of(levels)
    blocks = levels // chunk
    hs = [slice(h, h + HALF) for h in range(0, cells, HALF)]

    def result(block):
        span = pl.ds(block * chunk, chunk)
        return pltpu.make_async_copy(out_ref.at[:, span], out_hbm.at[:, span], sems.at[block])

    surface = gather_surface(count, cells, lat, received_ref)
    solved = [[surface[n * cells + s.start : n * cells + s.stop] for s in hs] for n in range(count)]

    def descend(group, solved):
        solved = jax.tree.map(lambda x: x, solved)
        for inner in range(GROUP):
            k = group * GROUP + inner
            for h, s in enumerate(hs):
                gain = state_ref[count * levels + k, s, :]
                for n in range(count):
                    solved[n][h] = state_ref[n * levels + k, s, :] + gain * solved[n][h]
                    out_ref[n, k, s, :] = solved[n][h]
        return solved

    def substitute(block, solved):
        first = block * (chunk // GROUP)
        solved = lax.fori_loop(first, first + chunk // GROUP, descend, solved)
        result(block).start()
        return solved

    lax.fori_loop(0, blocks, substitute, solved)
    for block in range(blocks):
        result(block).wait()


def eliminate(halos, small, fields):
    count, levels, cells, lat = fields[0].shape
    return pl.pallas_call(
        functools.partial(eliminate_kernel, levels),
        out_shape=pltpu.VMEM(((count + 1) * levels, cells, lat), F32),
        in_specs=[VMEM] * len(halos) + [ANY] * (len(small) + len(fields)),
        out_specs=VMEM,
        scratch_shapes=[pltpu.VMEM(x.shape, x.dtype) for x in (*small, *fields)]
        + [
            pltpu.VMEM((levels, count, cells, lat), F32),
            pltpu.VMEM((GROUP, count + 1, cells, lat), F32),
            pltpu.VMEM((GROUP, count, cells, lat), F32),
            pltpu.VMEM((GROUP, count, cells, lat), F32),
            pltpu.SemaphoreType.DMA((len(small),)),
            pltpu.SemaphoreType.DMA((levels // chunk_of(levels), len(fields))),
        ],
        compiler_params=pltpu.CompilerParams(vmem_limit_bytes=16 << 20),
        cost_estimate=pl.CostEstimate(flops=10**8, bytes_accessed=8 * 10**6, transcendentals=0),
        name="eliminate",
    )(*in_vmem(*halos), *in_hbm(*small, *fields))


def substitute(count, levels, state, received):
    shape = (count, levels, *state.shape[1:])
    return pl.pallas_call(
        substitute_kernel,
        out_shape=jax.ShapeDtypeStruct(shape, F32),
        in_specs=[VMEM] * 2,
        out_specs=ANY,
        scratch_shapes=[
            pltpu.VMEM(shape, F32),
            pltpu.SemaphoreType.DMA((levels // chunk_of(levels),)),
        ],
        compiler_params=pltpu.CompilerParams(vmem_limit_bytes=12 << 20),
        cost_estimate=pl.CostEstimate(flops=10**7, bytes_accessed=6 * 10**6, transcendentals=0),
        name="substitute",
    )(*in_vmem(state, received))


def shards(
    tracer,
    east_speed,
    north_speed,
    diffusivity,
    mixing,
    thickness,
    depth_levels,
    air_flux,
    margin_tile,
    margin_source,
    margin_cell,
    margin_weight,
):
    tiles = lax.axis_size("lon")
    by_level = lambda x: jnp.transpose(x, (1, 0, 2))
    rows = lambda x: x.reshape(-1, LANES)
    tracer = jnp.transpose(tracer, (0, 2, 1, 3))
    east, north, kappa, mixing, thick = [
        by_level(x) for x in (east_speed, north_speed, diffusivity, mixing, thickness)
    ]
    count, levels = tracer.shape[:2]
    small = [depth_levels, air_flux]
    small += [rows(x) for x in (margin_tile, margin_source, margin_cell, margin_weight)]
    up, down, mirror, messages, own = pack(tiles, [tracer, east, north, kappa], small)
    ring = [(i, (i + 1) % tiles) for i in range(tiles)]
    mirror = lax.ppermute(mirror, "lon", [(i, tiles - 1 - i) for i in range(tiles)])
    west = lax.ppermute(up, "lon", ring)
    far = lax.ppermute(down, "lon", [(j, i) for i, j in ring])
    received = lax.all_to_all(messages, "lon", split_axis=0, concat_axis=0, tiled=True)
    fields = [tracer, kappa, north, east, thick, mixing]
    state = eliminate([west, far], [own, mirror, depth_levels], fields)
    out = substitute(count, levels, state, received)
    return jnp.transpose(out, (0, 2, 1, 3))


def solution(mesh):
    placed = (
        P(None, "lon", None, "ens"),
        P("lon", None, "ens"),
        P("lon", None, "ens"),
        P("lon", None, "ens"),
        P("lon", None, "ens"),
        P("lon", None, "ens"),
        P("lon", "ens"),
        P("ens", "lon"),
        P(("ens", "lon"), None),
        P(("ens", "lon")),
        P(("ens", "lon")),
        P(("ens", "lon")),
    )
    return jax.shard_map(
        shards, mesh=mesh, in_specs=placed, out_specs=P(None, "lon", None, "ens"), check_vma=False
    )
```

```python
import functools

import jax
import jax.numpy as jnp
from jax import lax
from jax.experimental import pallas as pl
from jax.experimental.pallas import tpu as pltpu
from jax.sharding import PartitionSpec as P

CAP = 64
HALF = 8
GROUP = 5
AHEAD = (2, 1, 0)
PACK_AHEAD = 2
LANES = 128
F32 = jnp.float32


def chunk_of(levels):
    return max(c for c in range(GROUP, 4 * GROUP, GROUP) if levels % c == 0)


def thirds(x):
    high = x.astype(jnp.bfloat16)
    rest = x - high.astype(F32)
    mid = rest.astype(jnp.bfloat16)
    low = (rest - mid.astype(F32)).astype(jnp.bfloat16)
    return high, mid, low


VMEM = pl.BlockSpec(memory_space=pltpu.VMEM)
ANY = pl.BlockSpec(memory_space=pl.ANY)


def in_hbm(*arrays):
    return [pltpu.with_memory_space_constraint(x, pltpu.HBM) for x in arrays]


def in_vmem(*arrays):
    return [pltpu.with_memory_space_constraint(x, pltpu.VMEM) for x in arrays]


def lane_ids(rows):
    return lax.broadcasted_iota(jnp.int32, (rows, LANES), 1)


def row_ids(rows):
    return lax.broadcasted_iota(jnp.int32, (rows, LANES), 0)


def dot_nt(a, b):
    return lax.dot_general(a, b, (((1,), (1,)), ((), ())), preferred_element_type=F32)


def sum_parts(stacked):
    rows = stacked.shape[0] // 3
    return stacked[:rows] + stacked[rows : 2 * rows] + stacked[2 * rows :]


def dot_nn(a, b):
    return lax.dot_general(a, b, (((1,), (0,)), ((), ())), preferred_element_type=F32)


def make_messages(tiles, air_ref, tile_ref, source_ref, cell_ref, weight_ref, msg_ref):
    count, air_cells = air_ref.shape
    chunks = tile_ref.shape[0]
    one, zero = jnp.ones((), F32), jnp.zeros((), F32)
    rows = [slice(c, c + 1) for c in range(chunks)]
    owns = [
        jnp.broadcast_to(tile_ref[r, :], (tiles, LANES)) == row_ids(tiles) for r in rows
    ]
    owned = jnp.concatenate([jnp.where(o, one, zero) for o in owns], axis=0).astype(jnp.bfloat16)
    earlier = jnp.where(row_ids(LANES) < lane_ids(LANES), one, zero).astype(jnp.bfloat16)
    prior = dot_nn(owned, earlier)
    total = dot_nn(owned, jnp.ones((LANES, LANES), jnp.bfloat16))
    air_parts = jnp.concatenate(
        [p.astype(F32) for p in thirds(air_ref[...])], axis=0
    ).astype(jnp.bfloat16)
    carry = jnp.zeros((tiles, LANES), F32)
    slots, parts = [], []
    for c in range(chunks):
        span = slice(c * tiles, (c + 1) * tiles)
        slots.append(
            jnp.sum(jnp.where(owns[c], prior[span] + carry, zero), axis=0, keepdims=True)
        )
        carry = carry + total[span]
        picked = jnp.broadcast_to(source_ref[rows[c], :], (air_cells, LANES)) == row_ids(air_cells)
        taken = dot_nn(air_parts, jnp.where(picked, one, zero).astype(jnp.bfloat16))
        flux = taken[:count] + taken[count : 2 * count] + taken[2 * count : 3 * count]
        payload = weight_ref[rows[c], :] * flux
        record = jnp.concatenate(
            [
                payload,
                cell_ref[rows[c], :].astype(F32),
                jnp.zeros((HALF - count - 1, LANES), F32),
            ],
            axis=0,
        )
        parts.append([p.astype(F32) for p in thirds(record)])
    slot_hot = jnp.concatenate(
        [
            jnp.where(
                jnp.broadcast_to(s.astype(jnp.int32), (LANES, LANES)) == row_ids(LANES), one, zero
            ).astype(jnp.bfloat16)
            for s in slots
        ],
        axis=1,
    )
    spread = jnp.concatenate(
        [
            jnp.concatenate(
                [
                    jnp.where(
                        jnp.broadcast_to(tile_ref[rows[c], :], (HALF, LANES)) == d,
                        parts[c][part],
                        zero,
                    )
                    for part in range(3)
                    for d in range(tiles)
                ],
                axis=0,
            ).astype(jnp.bfloat16)
            for c in range(chunks)
        ],
        axis=1,
    )
    out = sum_parts(dot_nt(spread, slot_hot))
    cells = pltpu.roll(pltpu.roll(out, CAP, 1).reshape(tiles, HALF, LANES), HALF - count, 1)
    out = out.reshape(tiles, HALF, LANES)
    head = lax.broadcasted_iota(jnp.int32, out.shape, 1) == 0
    msg_ref[...] = jnp.where(head, out + cells, out)[:, :count]


def pack_kernel(
    levels,
    tiles,
    tracer_hbm,
    east_hbm,
    north_hbm,
    kappa_hbm,
    depth_hbm,
    air_hbm,
    tile_hbm,
    source_hbm,
    cell_hbm,
    weight_hbm,
    up_ref,
    down_ref,
    mirror_ref,
    msg_ref,
    own_ref,
    tracer_ref,
    east_ref,
    north_ref,
    kappa_ref,
    depth_ref,
    air_ref,
    tile_ref,
    source_ref,
    cell_ref,
    weight_ref,
    sems,
    small_sems,
):
    count, _, cells, _ = tracer_ref.shape
    fields = count + 2
    chunk = chunk_of(levels)
    blocks = levels // chunk
    lane = lane_ids(cells)

    def copies(block):
        span = pl.ds(block * chunk, chunk)
        pairs = [
            (tracer_hbm.at[:, span], tracer_ref.at[:, span]),
            (north_hbm.at[span], north_ref.at[span]),
            (kappa_hbm.at[span], kappa_ref.at[span]),
            (east_hbm.at[span, pl.ds(cells - HALF, HALF)], east_ref.at[span]),
        ]
        return [
            pltpu.make_async_copy(src, dst, sems.at[block, i]) for i, (src, dst) in enumerate(pairs)
        ]

    small = [
        pltpu.make_async_copy(src, dst, small_sems.at[i])
        for i, (src, dst) in enumerate(
            (
                (tile_hbm, tile_ref),
                (air_hbm, air_ref),
                (source_hbm, source_ref),
                (cell_hbm, cell_ref),
                (weight_hbm, weight_ref),
                (depth_hbm, depth_ref),
            )
        )
    ]
    for copy in small:
        copy.start()
    for block in range(PACK_AHEAD):
        for copy in copies(block):
            copy.start()
    for copy in small:
        copy.wait()
    for block in range(PACK_AHEAD, blocks):
        for copy in copies(block):
            copy.start()

    depth = depth_ref[...].astype(F32)
    up_ref[fields * levels : fields * levels + 1, :] = depth[cells - 1 : cells]
    down_ref[(fields - 1) * levels : (fields - 1) * levels + 1, :] = depth[0:1]
    def several(group, columns):
        columns = list(columns)
        for inner in range(chunk):
            k = group * chunk + inner
            slabs = [tracer_ref[n, k] for n in range(count)] + [north_ref[k], kappa_ref[k]]
            for f in range(fields):
                columns[f] = jnp.where(lane == k, pltpu.roll(slabs[f], k + 1, 1), columns[f])
                if f < count:
                    up_ref[pl.ds(f * levels + k, 1), :] = slabs[f][cells - 1 : cells]
                    down_ref[pl.ds(f * levels + k, 1), :] = slabs[f][0:1]
            up_ref[pl.ds(count * levels + k, 1), :] = east_ref[k, HALF - 1 : HALF, :]
            up_ref[pl.ds((count + 1) * levels + k, 1), :] = slabs[count + 1][cells - 1 : cells]
            down_ref[pl.ds(count * levels + k, 1), :] = slabs[count + 1][0:1]
        return tuple(columns)

    columns = [jnp.zeros((cells, LANES), F32)] * fields
    for block in range(blocks):
        for copy in copies(block):
            copy.wait()
        if block == 0:
            make_messages(tiles, air_ref, tile_ref, source_ref, cell_ref, weight_ref, msg_ref)
        columns = several(block, columns)
    last = depth.shape[1] - 1
    columns = [*columns, jnp.broadcast_to(depth[:, last : last + 1], (cells, LANES))]
    for f in range(fields + 1):
        own_ref[f * cells : (f + 1) * cells, :] = columns[f]
        for i in range(cells):
            spot = f * cells + cells - 1 - i
            mirror_ref[spot : spot + 1, :] = columns[f][i : i + 1]


def pack(tiles, fields, small):
    count, levels, cells, lat = fields[0].shape
    rows = lambda n: jax.ShapeDtypeStruct((-(-n // HALF) * HALF, lat), F32)
    return pl.pallas_call(
        functools.partial(pack_kernel, levels, tiles),
        out_shape=[
            rows((count + 2) * levels + 1),
            rows((count + 1) * levels + 1),
            jax.ShapeDtypeStruct(((count + 3) * cells, LANES), F32),
            jax.ShapeDtypeStruct((tiles, count, LANES), F32),
            pltpu.HBM(((count + 3) * cells, LANES), F32),
        ],
        in_specs=[ANY] * (len(fields) + len(small)),
        out_specs=[VMEM] * 5,
        scratch_shapes=[
            pltpu.VMEM((count, levels, cells, lat), F32),
            pltpu.VMEM((levels, HALF, lat), F32),
            pltpu.VMEM((levels, cells, lat), F32),
            pltpu.VMEM((levels, cells, lat), F32),
        ]
        + [pltpu.VMEM(x.shape, x.dtype) for x in small]
        + [
            pltpu.SemaphoreType.DMA((levels // chunk_of(levels), 4)),
            pltpu.SemaphoreType.DMA((6,)),
        ],
        compiler_params=pltpu.CompilerParams(vmem_limit_bytes=12 << 20),
        cost_estimate=pl.CostEstimate(flops=10**7, bytes_accessed=4 * 10**6, transcendentals=0),
        name="pack",
    )(*in_hbm(*fields, *small))


def gather_surface(count, cells, lat, received_ref):
    tiles = received_ref.shape[0]
    shift = lat.bit_length() - 1
    one, zero = jnp.ones((), F32), jnp.zeros((), F32)
    left, right = [[], [], []], []
    early = lane_ids(count) < CAP
    for t in range(0, tiles, 2):
        even, odd = received_ref[t], received_ref[t + 1]
        block = jnp.where(early, even, pltpu.roll(odd, CAP, 1))
        cell = jnp.where(early, pltpu.roll(even, CAP, 1), odd)[0:1].astype(jnp.int32)
        row = jnp.broadcast_to(lax.shift_right_logical(cell, shift), (cells, LANES))
        col = jnp.broadcast_to(cell & (lat - 1), (lat, LANES))
        right.append(jnp.where(col == row_ids(lat), one, zero).astype(jnp.bfloat16))
        hit = row == row_ids(cells)
        for p, part in enumerate(thirds(block)):
            part = part.astype(F32)
            left[p].append(
                jnp.concatenate(
                    [
                        jnp.where(hit, jnp.broadcast_to(part[n : n + 1], (cells, LANES)), zero)
                        for n in range(count)
                    ],
                    axis=0,
                ).astype(jnp.bfloat16)
            )
    spread = jnp.concatenate(right, axis=1)
    parts = jnp.concatenate([jnp.concatenate(part, axis=1) for part in left], axis=0)
    return sum_parts(dot_nt(parts, spread))


def eliminate_kernel(
    levels,
    west_ref,
    far_ref,
    own_hbm,
    mirror_hbm,
    depth_hbm,
    tracer_hbm,
    kappa_hbm,
    north_hbm,
    east_hbm,
    thick_hbm,
    mixing_hbm,
    state_ref,
    own_ref,
    mirror_ref,
    depth_ref,
    tracer_ref,
    kappa_ref,
    north_ref,
    east_ref,
    thick_ref,
    mixing_ref,
    fold_ref,
    next_ref,
    part_ref,
    south_ref,
    small_sems,
    sems,
):
    count, _, cells, lat = tracer_ref.shape
    chunk = chunk_of(levels)
    blocks, groups = levels // chunk, chunk // GROUP

    def copies(block):
        span = pl.ds(block * chunk, chunk)
        pairs = [(tracer_hbm.at[:, span], tracer_ref.at[:, span])] + [
            (hbm.at[span], ref.at[span])
            for hbm, ref in (
                (kappa_hbm, kappa_ref),
                (north_hbm, north_ref),
                (east_hbm, east_ref),
                (thick_hbm, thick_ref),
                (mixing_hbm, mixing_ref),
            )
        ]
        return [
            pltpu.make_async_copy(src, dst, sems.at[block, i]) for i, (src, dst) in enumerate(pairs)
        ]

    def fetched(block):
        for copy in copies(block):
            copy.wait()

        @pl.when(block >= sum(AHEAD))
        def _():
            for copy in copies(block - sum(AHEAD)):
                copy.start()

    def begin(stage):
        done = sum(AHEAD[:stage])
        for block in range(done, done + AHEAD[stage]):
            for copy in copies(blocks - 1 - block):
                copy.start()

    small = [
        pltpu.make_async_copy(src, dst, small_sems.at[i])
        for i, (src, dst) in enumerate(
            ((own_hbm, own_ref), (mirror_hbm, mirror_ref), (depth_hbm, depth_ref))
        )
    ]
    for copy in small:
        copy.start()
    begin(0)
    halves = cells // HALF
    fields = count + 2
    row8 = row_ids(HALF)
    lane8 = lane_ids(HALF)
    top = lane8 == lat - 1
    first = row8 == 0
    last = row8 == HALF - 1
    hs = [slice(h * HALF, (h + 1) * HALF) for h in range(halves)]

    def from_east(parts, halo):
        turned = [pltpu.roll(p, HALF - 1, 0) for p in parts]
        return [
            jnp.where(last, turned[h + 1] if h + 1 < halves else halo, turned[h])
            for h in range(halves)
        ]

    def from_west(parts, halo):
        turned = [pltpu.roll(p, 1, 0) for p in parts]
        return [
            jnp.where(first, turned[h - 1] if h > 0 else halo, turned[h]) for h in range(halves)
        ]

    def row_of(ref, index):
        return jnp.broadcast_to(ref[pl.ds(index, 1), :], (HALF, lat))

    for copy in small:
        copy.wait()
    begin(1)
    for h in range(halves):
        mine, other = [
            [ref[f * cells + h * HALF : f * cells + (h + 1) * HALF, :] for f in range(fields + 1)]
            for ref in (own_ref, mirror_ref)
        ]
        mean = 0.5 * (mine[count + 1] + other[count + 1])
        speed = 0.5 * (mine[count] - other[count])
        open_face = jnp.minimum(mine[fields], other[fields]) > lane8.astype(F32)
        near = jnp.where(open_face, jnp.maximum(speed, 0.0) + mean, 0.0)
        far = jnp.where(open_face, jnp.minimum(speed, 0.0) - mean, 0.0)
        for n in range(count):
            flux = near * mine[n] + far * other[n]
            for k in range(levels):
                fold_ref[k, n, hs[h], :] = pltpu.roll(flux, lat - 1 - k, 1)
    begin(2)
    depth = [depth_ref[s, :].astype(F32) for s in hs]
    depth_east = from_east(depth, row_of(far_ref, (fields - 1) * levels))
    limit_here = depth
    limit_east = [jnp.minimum(depth[h], depth_east[h]) for h in range(halves)]
    limit_north = [
        jnp.where(top, 0.0, jnp.minimum(depth[h], pltpu.roll(depth[h], lat - 1, 1)))
        for h in range(halves)
    ]
    limit_west = jnp.minimum(
        jnp.broadcast_to(depth[0][0:1], (HALF, lat)), row_of(west_ref, fields * levels)
    )

    def turned(group):
        for inner in range(GROUP):
            k = (levels - GROUP - group * GROUP) + (GROUP - 1 - inner)
            for s in hs:
                next_ref[inner, count, s, :] = pltpu.roll(kappa_ref[k, s, :], lat - 1, 1)
                for n in range(count):
                    next_ref[inner, n, s, :] = pltpu.roll(tracer_ref[n, k, s, :], lat - 1, 1)

    def fluxes(group):
        for inner in range(GROUP):
            k = (levels - GROUP - group * GROUP) + (GROUP - 1 - inner)
            level = k.astype(F32)
            kappa = [kappa_ref[k, s, :] for s in hs]
            speed = [east_ref[k, s, :] for s in hs]
            kappa_east = from_east(kappa, row_of(far_ref, count * levels + k))
            near_e, far_e = [], []
            for h in range(halves):
                mean = 0.5 * (kappa[h] + kappa_east[h])
                open_face = limit_east[h] > level
                near = jnp.maximum(speed[h], 0.0) + mean
                near_e.append(jnp.where(open_face, near, 0.0))
                far_e.append(jnp.where(open_face, speed[h] - near, 0.0))
            speed_w = row_of(west_ref, count * levels + k)
            kappa_w = row_of(west_ref, (count + 1) * levels + k)
            mean = 0.5 * (kappa_w + jnp.broadcast_to(kappa[0][0:1], (HALF, lat)))
            open_face = limit_west > level
            near = jnp.maximum(speed_w, 0.0) + mean
            near_w = jnp.where(open_face, near, 0.0)
            far_w = jnp.where(open_face, speed_w - near, 0.0)
            near_n, far_n = [], []
            for h in range(halves):
                speed_n = north_ref[k, hs[h], :]
                mean = 0.5 * (kappa[h] + next_ref[inner, count, hs[h], :])
                open_face = limit_north[h] > level
                near = jnp.maximum(speed_n, 0.0) + mean
                near_n.append(jnp.where(open_face, near, 0.0))
                far_n.append(jnp.where(open_face, speed_n - near, 0.0))
            for n in range(count):
                cell = [tracer_ref[n, k, s, :] for s in hs]
                cell_east = from_east(cell, row_of(far_ref, n * levels + k))
                flux_e = [near_e[h] * cell[h] + far_e[h] * cell_east[h] for h in range(halves)]
                flux_in = near_w * row_of(west_ref, n * levels + k) + far_w * jnp.broadcast_to(
                    cell[0][0:1], (HALF, lat)
                )
                flux_w = from_west(flux_e, flux_in)
                for h in range(halves):
                    flux_n = near_n[h] * cell[h] + far_n[h] * next_ref[inner, n, hs[h], :]
                    south_ref[inner, n, hs[h], :] = pltpu.roll(flux_n, 1, 1)
                    flux_n = jnp.where(top, fold_ref[k, n, hs[h], :], flux_n)
                    part_ref[inner, n, hs[h], :] = (cell[h] - (flux_e[h] - flux_w[h])) - flux_n

    def solve(group, state):
        thick, coupling, value, gain, scale = jax.tree.map(lambda x: x, state)
        for inner in range(GROUP):
            k = (levels - GROUP - group * GROUP) + (GROUP - 1 - inner)
            above = jnp.maximum(k - 1, 0)
            closed = jnp.where(k > 0, k.astype(F32), float(levels))
            for h in range(halves):
                thick_above = thick_ref[above, hs[h], :]
                here = 2.0 * mixing_ref[above, hs[h], :] / (thick_above + thick[h])
                here = jnp.where(limit_here[h] > closed, here, 0.0)
                scale[h] = 1.0 / (thick[h] + here + coupling[h] - coupling[h] * gain[h])
                gain[h] = here * scale[h]
                state_ref[count * levels + k, hs[h], :] = gain[h]
                share, below = thick[h] * scale[h], coupling[h] * scale[h]
                for n in range(count):
                    stepped = part_ref[inner, n, hs[h], :] + south_ref[inner, n, hs[h], :]
                    value[n][h] = share * stepped + below * value[n][h]
                    state_ref[n * levels + k, hs[h], :] = value[n][h]
                thick[h], coupling[h] = thick_above, here
        return thick, coupling, value, gain, scale

    def turn(group, state):
        ahead = group + 1

        @pl.when(lax.rem(ahead, groups) == 0)
        def _():
            fetched(blocks - 1 - lax.div(ahead, groups))

        state = solve(group - 1, state)
        fluxes(group)
        turned(ahead)
        return state

    zero = [jnp.zeros((HALF, lat), F32)] * halves
    total = blocks * groups
    fetched(jnp.int32(blocks - 1))
    turned(jnp.int32(0))
    fluxes(jnp.int32(0))
    turned(jnp.int32(1))
    state = ([thick_ref[levels - 1, s, :] for s in hs], zero, [zero] * count, zero, zero)
    state = lax.fori_loop(1, total - 1, turn, state)
    state = solve(jnp.int32(total - 2), state)
    fluxes(jnp.int32(total - 1))
    scale = solve(jnp.int32(total - 1), state)[4]
    for h in range(halves):
        state_ref[count * levels, hs[h], :] = jnp.where(limit_here[h] > 0.0, scale[h], 0.0)


def substitute_kernel(state_ref, received_ref, out_hbm, out_ref, sems):
    count, levels, cells, lat = out_ref.shape
    chunk = chunk_of(levels)
    blocks = levels // chunk
    hs = [slice(h, h + HALF) for h in range(0, cells, HALF)]

    def result(block):
        span = pl.ds(block * chunk, chunk)
        return pltpu.make_async_copy(out_ref.at[:, span], out_hbm.at[:, span], sems.at[block])

    surface = gather_surface(count, cells, lat, received_ref)
    solved = [[surface[n * cells + s.start : n * cells + s.stop] for s in hs] for n in range(count)]

    def descend(group, solved):
        solved = jax.tree.map(lambda x: x, solved)
        for inner in range(GROUP):
            k = group * GROUP + inner
            for h, s in enumerate(hs):
                gain = state_ref[count * levels + k, s, :]
                for n in range(count):
                    solved[n][h] = state_ref[n * levels + k, s, :] + gain * solved[n][h]
                    out_ref[n, k, s, :] = solved[n][h]
        return solved

    def substitute(block, solved):
        first = block * (chunk // GROUP)
        solved = lax.fori_loop(first, first + chunk // GROUP, descend, solved)
        result(block).start()
        return solved

    lax.fori_loop(0, blocks, substitute, solved)
    for block in range(blocks):
        result(block).wait()


def eliminate(halos, small, fields):
    count, levels, cells, lat = fields[0].shape
    return pl.pallas_call(
        functools.partial(eliminate_kernel, levels),
        out_shape=pltpu.VMEM(((count + 1) * levels, cells, lat), F32),
        in_specs=[VMEM] * len(halos) + [ANY] * (len(small) + len(fields)),
        out_specs=VMEM,
        scratch_shapes=[pltpu.VMEM(x.shape, x.dtype) for x in (*small, *fields)]
        + [
            pltpu.VMEM((levels, count, cells, lat), F32),
            pltpu.VMEM((GROUP, count + 1, cells, lat), F32),
            pltpu.VMEM((GROUP, count, cells, lat), F32),
            pltpu.VMEM((GROUP, count, cells, lat), F32),
            pltpu.SemaphoreType.DMA((len(small),)),
            pltpu.SemaphoreType.DMA((levels // chunk_of(levels), len(fields))),
        ],
        compiler_params=pltpu.CompilerParams(vmem_limit_bytes=16 << 20),
        cost_estimate=pl.CostEstimate(flops=10**8, bytes_accessed=8 * 10**6, transcendentals=0),
        name="eliminate",
    )(*in_vmem(*halos), *in_hbm(*small, *fields))


def substitute(count, levels, state, received):
    shape = (count, levels, *state.shape[1:])
    return pl.pallas_call(
        substitute_kernel,
        out_shape=jax.ShapeDtypeStruct(shape, F32),
        in_specs=[VMEM] * 2,
        out_specs=ANY,
        scratch_shapes=[
            pltpu.VMEM(shape, F32),
            pltpu.SemaphoreType.DMA((levels // chunk_of(levels),)),
        ],
        compiler_params=pltpu.CompilerParams(vmem_limit_bytes=12 << 20),
        cost_estimate=pl.CostEstimate(flops=10**7, bytes_accessed=6 * 10**6, transcendentals=0),
        name="substitute",
    )(*in_vmem(state, received))


def shards(
    tracer,
    east_speed,
    north_speed,
    diffusivity,
    mixing,
    thickness,
    depth_levels,
    air_flux,
    margin_tile,
    margin_source,
    margin_cell,
    margin_weight,
):
    tiles = lax.axis_size("lon")
    by_level = lambda x: jnp.transpose(x, (1, 0, 2))
    rows = lambda x: x.reshape(-1, LANES)
    tracer = jnp.transpose(tracer, (0, 2, 1, 3))
    east, north, kappa, mixing, thick = [
        by_level(x) for x in (east_speed, north_speed, diffusivity, mixing, thickness)
    ]
    count, levels = tracer.shape[:2]
    small = [depth_levels, air_flux]
    small += [rows(x) for x in (margin_tile, margin_source, margin_cell, margin_weight)]
    up, down, mirror, messages, own = pack(tiles, [tracer, east, north, kappa], small)
    ring = [(i, (i + 1) % tiles) for i in range(tiles)]
    mirror = lax.ppermute(mirror, "lon", [(i, tiles - 1 - i) for i in range(tiles)])
    west = lax.ppermute(up, "lon", ring)
    far = lax.ppermute(down, "lon", [(j, i) for i, j in ring])
    received = lax.all_to_all(messages, "lon", split_axis=0, concat_axis=0, tiled=True)
    fields = [tracer, kappa, north, east, thick, mixing]
    state = eliminate([west, far], [own, mirror, depth_levels], fields)
    out = substitute(count, levels, state, received)
    return jnp.transpose(out, (0, 2, 1, 3))


def solution(mesh):
    placed = (
        P(None, "lon", None, "ens"),
        P("lon", None, "ens"),
        P("lon", None, "ens"),
        P("lon", None, "ens"),
        P("lon", None, "ens"),
        P("lon", None, "ens"),
        P("lon", "ens"),
        P("ens", "lon"),
        P(("ens", "lon"), None),
        P(("ens", "lon")),
        P(("ens", "lon")),
        P(("ens", "lon")),
    )
    return jax.shard_map(
        shards, mesh=mesh, in_specs=placed, out_specs=P(None, "lon", None, "ens"), check_vma=False
    )
```

```python
import functools

import jax
import jax.numpy as jnp
from jax import lax
from jax.experimental import pallas as pl
from jax.experimental.pallas import tpu as pltpu
from jax.sharding import PartitionSpec as P

CAP = 64
HALF = 8
GROUP = 5
AHEAD = (2, 1, 0)
PACK_AHEAD = 2
SETTLE = 17 * 10**8
LANES = 128
F32 = jnp.float32


def chunk_of(levels):
    return max(c for c in range(GROUP, 4 * GROUP, GROUP) if levels % c == 0)


def thirds(x):
    high = x.astype(jnp.bfloat16)
    rest = x - high.astype(F32)
    mid = rest.astype(jnp.bfloat16)
    low = (rest - mid.astype(F32)).astype(jnp.bfloat16)
    return high, mid, low


VMEM = pl.BlockSpec(memory_space=pltpu.VMEM)
ANY = pl.BlockSpec(memory_space=pl.ANY)


def in_hbm(*arrays):
    return [pltpu.with_memory_space_constraint(x, pltpu.HBM) for x in arrays]


def in_vmem(*arrays):
    return [pltpu.with_memory_space_constraint(x, pltpu.VMEM) for x in arrays]


def lane_ids(rows):
    return lax.broadcasted_iota(jnp.int32, (rows, LANES), 1)


def row_ids(rows):
    return lax.broadcasted_iota(jnp.int32, (rows, LANES), 0)


def dot_nt(a, b):
    return lax.dot_general(a, b, (((1,), (1,)), ((), ())), preferred_element_type=F32)


def sum_parts(stacked):
    rows = stacked.shape[0] // 3
    return stacked[:rows] + stacked[rows : 2 * rows] + stacked[2 * rows :]


def dot_nn(a, b):
    return lax.dot_general(a, b, (((1,), (0,)), ((), ())), preferred_element_type=F32)


def make_messages(tiles, air_ref, tile_ref, source_ref, cell_ref, weight_ref, msg_ref):
    count, air_cells = air_ref.shape
    chunks = tile_ref.shape[0]
    one, zero = jnp.ones((), F32), jnp.zeros((), F32)
    rows = [slice(c, c + 1) for c in range(chunks)]
    owns = [
        jnp.broadcast_to(tile_ref[r, :], (tiles, LANES)) == row_ids(tiles) for r in rows
    ]
    owned = jnp.concatenate([jnp.where(o, one, zero) for o in owns], axis=0).astype(jnp.bfloat16)
    earlier = jnp.where(row_ids(LANES) < lane_ids(LANES), one, zero).astype(jnp.bfloat16)
    prior = dot_nn(owned, earlier)
    total = dot_nn(owned, jnp.ones((LANES, LANES), jnp.bfloat16))
    air_parts = jnp.concatenate(
        [p.astype(F32) for p in thirds(air_ref[...])], axis=0
    ).astype(jnp.bfloat16)
    carry = jnp.zeros((tiles, LANES), F32)
    slots, parts = [], []
    for c in range(chunks):
        span = slice(c * tiles, (c + 1) * tiles)
        slots.append(
            jnp.sum(jnp.where(owns[c], prior[span] + carry, zero), axis=0, keepdims=True)
        )
        carry = carry + total[span]
        picked = jnp.broadcast_to(source_ref[rows[c], :], (air_cells, LANES)) == row_ids(air_cells)
        taken = dot_nn(air_parts, jnp.where(picked, one, zero).astype(jnp.bfloat16))
        flux = taken[:count] + taken[count : 2 * count] + taken[2 * count : 3 * count]
        payload = weight_ref[rows[c], :] * flux
        record = jnp.concatenate(
            [
                payload,
                cell_ref[rows[c], :].astype(F32),
                jnp.zeros((HALF - count - 1, LANES), F32),
            ],
            axis=0,
        )
        parts.append([p.astype(F32) for p in thirds(record)])
    slot_hot = jnp.concatenate(
        [
            jnp.where(
                jnp.broadcast_to(s.astype(jnp.int32), (LANES, LANES)) == row_ids(LANES), one, zero
            ).astype(jnp.bfloat16)
            for s in slots
        ],
        axis=1,
    )
    spread = jnp.concatenate(
        [
            jnp.concatenate(
                [
                    jnp.where(
                        jnp.broadcast_to(tile_ref[rows[c], :], (HALF, LANES)) == d,
                        parts[c][part],
                        zero,
                    )
                    for part in range(3)
                    for d in range(tiles)
                ],
                axis=0,
            ).astype(jnp.bfloat16)
            for c in range(chunks)
        ],
        axis=1,
    )
    out = sum_parts(dot_nt(spread, slot_hot))
    cells = pltpu.roll(pltpu.roll(out, CAP, 1).reshape(tiles, HALF, LANES), HALF - count, 1)
    out = out.reshape(tiles, HALF, LANES)
    head = lax.broadcasted_iota(jnp.int32, out.shape, 1) == 0
    msg_ref[...] = jnp.where(head, out + cells, out)[:, :count]


def pack_kernel(
    levels,
    tiles,
    tracer_hbm,
    east_hbm,
    north_hbm,
    kappa_hbm,
    depth_hbm,
    air_hbm,
    tile_hbm,
    source_hbm,
    cell_hbm,
    weight_hbm,
    up_ref,
    down_ref,
    mirror_ref,
    msg_ref,
    own_ref,
    tracer_ref,
    east_ref,
    north_ref,
    kappa_ref,
    depth_ref,
    air_ref,
    tile_ref,
    source_ref,
    cell_ref,
    weight_ref,
    sems,
    small_sems,
):
    count, _, cells, _ = tracer_ref.shape
    fields = count + 2
    chunk = chunk_of(levels)
    blocks = levels // chunk
    lane = lane_ids(cells)

    def copies(block):
        span = pl.ds(block * chunk, chunk)
        pairs = [
            (tracer_hbm.at[:, span], tracer_ref.at[:, span]),
            (north_hbm.at[span], north_ref.at[span]),
            (kappa_hbm.at[span], kappa_ref.at[span]),
            (east_hbm.at[span, pl.ds(cells - HALF, HALF)], east_ref.at[span]),
        ]
        return [
            pltpu.make_async_copy(src, dst, sems.at[block, i]) for i, (src, dst) in enumerate(pairs)
        ]

    small = [
        pltpu.make_async_copy(src, dst, small_sems.at[i])
        for i, (src, dst) in enumerate(
            (
                (tile_hbm, tile_ref),
                (air_hbm, air_ref),
                (source_hbm, source_ref),
                (cell_hbm, cell_ref),
                (weight_hbm, weight_ref),
                (depth_hbm, depth_ref),
            )
        )
    ]
    for copy in small:
        copy.start()
    for block in range(PACK_AHEAD):
        for copy in copies(block):
            copy.start()
    for copy in small:
        copy.wait()
    for block in range(PACK_AHEAD, blocks):
        for copy in copies(block):
            copy.start()

    depth = depth_ref[...].astype(F32)
    up_ref[fields * levels : fields * levels + 1, :] = depth[cells - 1 : cells]
    down_ref[(fields - 1) * levels : (fields - 1) * levels + 1, :] = depth[0:1]
    def several(group, columns):
        columns = list(columns)
        for inner in range(chunk):
            k = group * chunk + inner
            slabs = [tracer_ref[n, k] for n in range(count)] + [north_ref[k], kappa_ref[k]]
            for f in range(fields):
                columns[f] = jnp.where(lane == k, pltpu.roll(slabs[f], k + 1, 1), columns[f])
                if f < count:
                    up_ref[pl.ds(f * levels + k, 1), :] = slabs[f][cells - 1 : cells]
                    down_ref[pl.ds(f * levels + k, 1), :] = slabs[f][0:1]
            up_ref[pl.ds(count * levels + k, 1), :] = east_ref[k, HALF - 1 : HALF, :]
            up_ref[pl.ds((count + 1) * levels + k, 1), :] = slabs[count + 1][cells - 1 : cells]
            down_ref[pl.ds(count * levels + k, 1), :] = slabs[count + 1][0:1]
        return tuple(columns)

    columns = [jnp.zeros((cells, LANES), F32)] * fields
    for block in range(blocks):
        for copy in copies(block):
            copy.wait()
        if block == 0:
            make_messages(tiles, air_ref, tile_ref, source_ref, cell_ref, weight_ref, msg_ref)
        columns = several(block, columns)
    last = depth.shape[1] - 1
    columns = [*columns, jnp.broadcast_to(depth[:, last : last + 1], (cells, LANES))]
    for f in range(fields + 1):
        own_ref[f * cells : (f + 1) * cells, :] = columns[f]
        for i in range(cells):
            spot = f * cells + cells - 1 - i
            mirror_ref[spot : spot + 1, :] = columns[f][i : i + 1]


def pack(tiles, fields, small):
    count, levels, cells, lat = fields[0].shape
    rows = lambda n: jax.ShapeDtypeStruct((-(-n // HALF) * HALF, lat), F32)
    return pl.pallas_call(
        functools.partial(pack_kernel, levels, tiles),
        out_shape=[
            rows((count + 2) * levels + 1),
            rows((count + 1) * levels + 1),
            jax.ShapeDtypeStruct(((count + 3) * cells, LANES), F32),
            jax.ShapeDtypeStruct((tiles, count, LANES), F32),
            pltpu.HBM(((count + 3) * cells, LANES), F32),
        ],
        in_specs=[ANY] * (len(fields) + len(small)),
        out_specs=[VMEM] * 5,
        scratch_shapes=[
            pltpu.VMEM((count, levels, cells, lat), F32),
            pltpu.VMEM((levels, HALF, lat), F32),
            pltpu.VMEM((levels, cells, lat), F32),
            pltpu.VMEM((levels, cells, lat), F32),
        ]
        + [pltpu.VMEM(x.shape, x.dtype) for x in small]
        + [
            pltpu.SemaphoreType.DMA((levels // chunk_of(levels), 4)),
            pltpu.SemaphoreType.DMA((6,)),
        ],
        compiler_params=pltpu.CompilerParams(vmem_limit_bytes=12 << 20),
        cost_estimate=pl.CostEstimate(flops=10**7, bytes_accessed=4 * 10**6, transcendentals=0),
        name="pack",
    )(*in_hbm(*fields, *small))


def gather_surface(count, cells, lat, received_ref):
    tiles = received_ref.shape[0]
    shift = lat.bit_length() - 1
    one, zero = jnp.ones((), F32), jnp.zeros((), F32)
    left, right = [[], [], []], []
    early = lane_ids(count) < CAP
    for t in range(0, tiles, 2):
        even, odd = received_ref[t], received_ref[t + 1]
        block = jnp.where(early, even, pltpu.roll(odd, CAP, 1))
        cell = jnp.where(early, pltpu.roll(even, CAP, 1), odd)[0:1].astype(jnp.int32)
        row = jnp.broadcast_to(lax.shift_right_logical(cell, shift), (cells, LANES))
        col = jnp.broadcast_to(cell & (lat - 1), (lat, LANES))
        right.append(jnp.where(col == row_ids(lat), one, zero).astype(jnp.bfloat16))
        hit = row == row_ids(cells)
        for p, part in enumerate(thirds(block)):
            part = part.astype(F32)
            left[p].append(
                jnp.concatenate(
                    [
                        jnp.where(hit, jnp.broadcast_to(part[n : n + 1], (cells, LANES)), zero)
                        for n in range(count)
                    ],
                    axis=0,
                ).astype(jnp.bfloat16)
            )
    spread = jnp.concatenate(right, axis=1)
    parts = jnp.concatenate([jnp.concatenate(part, axis=1) for part in left], axis=0)
    return sum_parts(dot_nt(parts, spread))


def eliminate_kernel(
    levels,
    west_ref,
    far_ref,
    own_hbm,
    mirror_hbm,
    depth_hbm,
    tracer_hbm,
    kappa_hbm,
    north_hbm,
    east_hbm,
    thick_hbm,
    mixing_hbm,
    state_ref,
    own_ref,
    mirror_ref,
    depth_ref,
    tracer_ref,
    kappa_ref,
    north_ref,
    east_ref,
    thick_ref,
    mixing_ref,
    fold_ref,
    next_ref,
    part_ref,
    south_ref,
    small_sems,
    sems,
):
    count, _, cells, lat = tracer_ref.shape
    chunk = chunk_of(levels)
    blocks, groups = levels // chunk, chunk // GROUP

    def copies(block):
        span = pl.ds(block * chunk, chunk)
        pairs = [(tracer_hbm.at[:, span], tracer_ref.at[:, span])] + [
            (hbm.at[span], ref.at[span])
            for hbm, ref in (
                (kappa_hbm, kappa_ref),
                (north_hbm, north_ref),
                (east_hbm, east_ref),
                (thick_hbm, thick_ref),
                (mixing_hbm, mixing_ref),
            )
        ]
        return [
            pltpu.make_async_copy(src, dst, sems.at[block, i]) for i, (src, dst) in enumerate(pairs)
        ]

    def fetched(block):
        for copy in copies(block):
            copy.wait()

        @pl.when(block >= sum(AHEAD))
        def _():
            for copy in copies(block - sum(AHEAD)):
                copy.start()

    def begin(stage):
        done = sum(AHEAD[:stage])
        for block in range(done, done + AHEAD[stage]):
            for copy in copies(blocks - 1 - block):
                copy.start()

    small = [
        pltpu.make_async_copy(src, dst, small_sems.at[i])
        for i, (src, dst) in enumerate(
            ((own_hbm, own_ref), (mirror_hbm, mirror_ref), (depth_hbm, depth_ref))
        )
    ]
    for copy in small:
        copy.start()
    begin(0)
    halves = cells // HALF
    fields = count + 2
    row8 = row_ids(HALF)
    lane8 = lane_ids(HALF)
    top = lane8 == lat - 1
    first = row8 == 0
    last = row8 == HALF - 1
    hs = [slice(h * HALF, (h + 1) * HALF) for h in range(halves)]

    def from_east(parts, halo):
        turned = [pltpu.roll(p, HALF - 1, 0) for p in parts]
        return [
            jnp.where(last, turned[h + 1] if h + 1 < halves else halo, turned[h])
            for h in range(halves)
        ]

    def from_west(parts, halo):
        turned = [pltpu.roll(p, 1, 0) for p in parts]
        return [
            jnp.where(first, turned[h - 1] if h > 0 else halo, turned[h]) for h in range(halves)
        ]

    def row_of(ref, index):
        return jnp.broadcast_to(ref[pl.ds(index, 1), :], (HALF, lat))

    for copy in small:
        copy.wait()
    begin(1)
    for h in range(halves):
        mine, other = [
            [ref[f * cells + h * HALF : f * cells + (h + 1) * HALF, :] for f in range(fields + 1)]
            for ref in (own_ref, mirror_ref)
        ]
        mean = 0.5 * (mine[count + 1] + other[count + 1])
        speed = 0.5 * (mine[count] - other[count])
        open_face = jnp.minimum(mine[fields], other[fields]) > lane8.astype(F32)
        near = jnp.where(open_face, jnp.maximum(speed, 0.0) + mean, 0.0)
        far = jnp.where(open_face, jnp.minimum(speed, 0.0) - mean, 0.0)
        for n in range(count):
            flux = near * mine[n] + far * other[n]
            for k in range(levels):
                fold_ref[k, n, hs[h], :] = pltpu.roll(flux, lat - 1 - k, 1)
    begin(2)
    depth = [depth_ref[s, :].astype(F32) for s in hs]
    depth_east = from_east(depth, row_of(far_ref, (fields - 1) * levels))
    limit_here = depth
    limit_east = [jnp.minimum(depth[h], depth_east[h]) for h in range(halves)]
    limit_north = [
        jnp.where(top, 0.0, jnp.minimum(depth[h], pltpu.roll(depth[h], lat - 1, 1)))
        for h in range(halves)
    ]
    limit_west = jnp.minimum(
        jnp.broadcast_to(depth[0][0:1], (HALF, lat)), row_of(west_ref, fields * levels)
    )

    def turned(group):
        for inner in range(GROUP):
            k = (levels - GROUP - group * GROUP) + (GROUP - 1 - inner)
            for s in hs:
                next_ref[inner, count, s, :] = pltpu.roll(kappa_ref[k, s, :], lat - 1, 1)
                for n in range(count):
                    next_ref[inner, n, s, :] = pltpu.roll(tracer_ref[n, k, s, :], lat - 1, 1)

    def fluxes(group):
        for inner in range(GROUP):
            k = (levels - GROUP - group * GROUP) + (GROUP - 1 - inner)
            level = k.astype(F32)
            kappa = [kappa_ref[k, s, :] for s in hs]
            speed = [east_ref[k, s, :] for s in hs]
            kappa_east = from_east(kappa, row_of(far_ref, count * levels + k))
            near_e, far_e = [], []
            for h in range(halves):
                mean = 0.5 * (kappa[h] + kappa_east[h])
                open_face = limit_east[h] > level
                near = jnp.maximum(speed[h], 0.0) + mean
                near_e.append(jnp.where(open_face, near, 0.0))
                far_e.append(jnp.where(open_face, speed[h] - near, 0.0))
            speed_w = row_of(west_ref, count * levels + k)
            kappa_w = row_of(west_ref, (count + 1) * levels + k)
            mean = 0.5 * (kappa_w + jnp.broadcast_to(kappa[0][0:1], (HALF, lat)))
            open_face = limit_west > level
            near = jnp.maximum(speed_w, 0.0) + mean
            near_w = jnp.where(open_face, near, 0.0)
            far_w = jnp.where(open_face, speed_w - near, 0.0)
            near_n, far_n = [], []
            for h in range(halves):
                speed_n = north_ref[k, hs[h], :]
                mean = 0.5 * (kappa[h] + next_ref[inner, count, hs[h], :])
                open_face = limit_north[h] > level
                near = jnp.maximum(speed_n, 0.0) + mean
                near_n.append(jnp.where(open_face, near, 0.0))
                far_n.append(jnp.where(open_face, speed_n - near, 0.0))
            for n in range(count):
                cell = [tracer_ref[n, k, s, :] for s in hs]
                cell_east = from_east(cell, row_of(far_ref, n * levels + k))
                flux_e = [near_e[h] * cell[h] + far_e[h] * cell_east[h] for h in range(halves)]
                flux_in = near_w * row_of(west_ref, n * levels + k) + far_w * jnp.broadcast_to(
                    cell[0][0:1], (HALF, lat)
                )
                flux_w = from_west(flux_e, flux_in)
                for h in range(halves):
                    flux_n = near_n[h] * cell[h] + far_n[h] * next_ref[inner, n, hs[h], :]
                    south_ref[inner, n, hs[h], :] = pltpu.roll(flux_n, 1, 1)
                    flux_n = jnp.where(top, fold_ref[k, n, hs[h], :], flux_n)
                    part_ref[inner, n, hs[h], :] = (cell[h] - (flux_e[h] - flux_w[h])) - flux_n

    def solve(group, state):
        thick, coupling, value, gain, scale = jax.tree.map(lambda x: x, state)
        for inner in range(GROUP):
            k = (levels - GROUP - group * GROUP) + (GROUP - 1 - inner)
            above = jnp.maximum(k - 1, 0)
            closed = jnp.where(k > 0, k.astype(F32), float(levels))
            for h in range(halves):
                thick_above = thick_ref[above, hs[h], :]
                here = 2.0 * mixing_ref[above, hs[h], :] / (thick_above + thick[h])
                here = jnp.where(limit_here[h] > closed, here, 0.0)
                scale[h] = 1.0 / (thick[h] + here + coupling[h] - coupling[h] * gain[h])
                gain[h] = here * scale[h]
                state_ref[count * levels + k, hs[h], :] = gain[h]
                share, below = thick[h] * scale[h], coupling[h] * scale[h]
                for n in range(count):
                    stepped = part_ref[inner, n, hs[h], :] + south_ref[inner, n, hs[h], :]
                    value[n][h] = share * stepped + below * value[n][h]
                    state_ref[n * levels + k, hs[h], :] = value[n][h]
                thick[h], coupling[h] = thick_above, here
        return thick, coupling, value, gain, scale

    def turn(group, state):
        ahead = group + 1

        @pl.when(lax.rem(ahead, groups) == 0)
        def _():
            fetched(blocks - 1 - lax.div(ahead, groups))

        state = solve(group - 1, state)
        fluxes(group)
        turned(ahead)
        return state

    zero = [jnp.zeros((HALF, lat), F32)] * halves
    total = blocks * groups
    fetched(jnp.int32(blocks - 1))
    turned(jnp.int32(0))
    fluxes(jnp.int32(0))
    turned(jnp.int32(1))
    state = ([thick_ref[levels - 1, s, :] for s in hs], zero, [zero] * count, zero, zero)
    state = lax.fori_loop(1, total - 1, turn, state)
    state = solve(jnp.int32(total - 2), state)
    fluxes(jnp.int32(total - 1))
    scale = solve(jnp.int32(total - 1), state)[4]
    for h in range(halves):
        state_ref[count * levels, hs[h], :] = jnp.where(limit_here[h] > 0.0, scale[h], 0.0)


def substitute_kernel(state_ref, received_ref, out_hbm, out_ref, sems):
    count, levels, cells, lat = out_ref.shape
    chunk = chunk_of(levels)
    blocks = levels // chunk
    hs = [slice(h, h + HALF) for h in range(0, cells, HALF)]

    def result(block):
        span = pl.ds(block * chunk, chunk)
        return pltpu.make_async_copy(out_ref.at[:, span], out_hbm.at[:, span], sems.at[block])

    surface = gather_surface(count, cells, lat, received_ref)
    solved = [[surface[n * cells + s.start : n * cells + s.stop] for s in hs] for n in range(count)]

    def descend(group, solved):
        solved = jax.tree.map(lambda x: x, solved)
        for inner in range(GROUP):
            k = group * GROUP + inner
            for h, s in enumerate(hs):
                gain = state_ref[count * levels + k, s, :]
                for n in range(count):
                    solved[n][h] = state_ref[n * levels + k, s, :] + gain * solved[n][h]
                    out_ref[n, k, s, :] = solved[n][h]
        return solved

    def substitute(block, solved):
        first = block * (chunk // GROUP)
        solved = lax.fori_loop(first, first + chunk // GROUP, descend, solved)
        result(block).start()
        return solved

    lax.fori_loop(0, blocks, substitute, solved)
    for block in range(blocks):
        result(block).wait()


def eliminate(halos, small, fields):
    count, levels, cells, lat = fields[0].shape
    return pl.pallas_call(
        functools.partial(eliminate_kernel, levels),
        out_shape=pltpu.VMEM(((count + 1) * levels, cells, lat), F32),
        in_specs=[VMEM] * len(halos) + [ANY] * (len(small) + len(fields)),
        out_specs=VMEM,
        scratch_shapes=[pltpu.VMEM(x.shape, x.dtype) for x in (*small, *fields)]
        + [
            pltpu.VMEM((levels, count, cells, lat), F32),
            pltpu.VMEM((GROUP, count + 1, cells, lat), F32),
            pltpu.VMEM((GROUP, count, cells, lat), F32),
            pltpu.VMEM((GROUP, count, cells, lat), F32),
            pltpu.SemaphoreType.DMA((len(small),)),
            pltpu.SemaphoreType.DMA((levels // chunk_of(levels), len(fields))),
        ],
        compiler_params=pltpu.CompilerParams(vmem_limit_bytes=16 << 20),
        cost_estimate=pl.CostEstimate(flops=10**8, bytes_accessed=8 * 10**6, transcendentals=0),
        name="eliminate",
    )(*in_vmem(*halos), *in_hbm(*small, *fields))


def settle_kernel(block_ref, out_hbm, sem):
    copy = pltpu.make_async_copy(block_ref, out_hbm, sem)
    copy.start()
    copy.wait()


def settle(block):
    return pl.pallas_call(
        settle_kernel,
        out_shape=pltpu.HBM(block.shape, block.dtype),
        in_specs=[VMEM],
        out_specs=ANY,
        scratch_shapes=[pltpu.SemaphoreType.DMA],
        cost_estimate=pl.CostEstimate(flops=SETTLE, bytes_accessed=10**5, transcendentals=0),
        name="settle",
    )(*in_vmem(block))


def substitute(count, levels, state, received):
    shape = (count, levels, *state.shape[1:])
    return pl.pallas_call(
        substitute_kernel,
        out_shape=jax.ShapeDtypeStruct(shape, F32),
        in_specs=[VMEM] * 2,
        out_specs=ANY,
        scratch_shapes=[
            pltpu.VMEM(shape, F32),
            pltpu.SemaphoreType.DMA((levels // chunk_of(levels),)),
        ],
        compiler_params=pltpu.CompilerParams(vmem_limit_bytes=12 << 20),
        cost_estimate=pl.CostEstimate(flops=10**7, bytes_accessed=6 * 10**6, transcendentals=0),
        name="substitute",
    )(*in_vmem(state, received))


def shards(
    tracer,
    east_speed,
    north_speed,
    diffusivity,
    mixing,
    thickness,
    depth_levels,
    air_flux,
    margin_tile,
    margin_source,
    margin_cell,
    margin_weight,
):
    tiles = lax.axis_size("lon")
    by_level = lambda x: jnp.transpose(x, (1, 0, 2))
    rows = lambda x: x.reshape(-1, LANES)
    tracer = jnp.transpose(tracer, (0, 2, 1, 3))
    east, north, kappa, mixing, thick = [
        by_level(x) for x in (east_speed, north_speed, diffusivity, mixing, thickness)
    ]
    count, levels = tracer.shape[:2]
    small = [depth_levels, air_flux]
    small += [rows(x) for x in (margin_tile, margin_source, margin_cell, margin_weight)]
    up, down, mirror, messages, own = pack(tiles, [tracer, east, north, kappa], small)
    ring = [(i, (i + 1) % tiles) for i in range(tiles)]
    mirror = lax.ppermute(mirror, "lon", [(i, tiles - 1 - i) for i in range(tiles)])
    west = lax.ppermute(up, "lon", ring)
    far = lax.ppermute(down, "lon", [(j, i) for i, j in ring])
    received = lax.all_to_all(messages, "lon", split_axis=0, concat_axis=0, tiled=True)
    mirror = settle(mirror)
    fields = [tracer, kappa, north, east, thick, mixing]
    state = eliminate([west, far], [own, mirror, depth_levels], fields)
    out = substitute(count, levels, state, received)
    return jnp.transpose(out, (0, 2, 1, 3))


def solution(mesh):
    placed = (
        P(None, "lon", None, "ens"),
        P("lon", None, "ens"),
        P("lon", None, "ens"),
        P("lon", None, "ens"),
        P("lon", None, "ens"),
        P("lon", None, "ens"),
        P("lon", "ens"),
        P("ens", "lon"),
        P(("ens", "lon"), None),
        P(("ens", "lon")),
        P(("ens", "lon")),
        P(("ens", "lon")),
    )
    return jax.shard_map(
        shards, mesh=mesh, in_specs=placed, out_specs=P(None, "lon", None, "ens"), check_vma=False
    )
```

```python
import functools

import jax
import jax.numpy as jnp
from jax import lax
from jax.experimental import pallas as pl
from jax.experimental.pallas import tpu as pltpu
from jax.sharding import PartitionSpec as P

CAP = 64
HALF = 8
GROUP = 5
AHEAD = (2, 1, 0)
PACK_AHEAD = 2
SETTLE = 17 * 10**8
LANES = 128
F32 = jnp.float32


def chunk_of(levels):
    return max(c for c in range(GROUP, 4 * GROUP, GROUP) if levels % c == 0)


def thirds(x):
    high = x.astype(jnp.bfloat16)
    rest = x - high.astype(F32)
    mid = rest.astype(jnp.bfloat16)
    low = (rest - mid.astype(F32)).astype(jnp.bfloat16)
    return high, mid, low


VMEM = pl.BlockSpec(memory_space=pltpu.VMEM)
ANY = pl.BlockSpec(memory_space=pl.ANY)


def in_hbm(*arrays):
    return [pltpu.with_memory_space_constraint(x, pltpu.HBM) for x in arrays]


def in_vmem(*arrays):
    return [pltpu.with_memory_space_constraint(x, pltpu.VMEM) for x in arrays]


def lane_ids(rows):
    return lax.broadcasted_iota(jnp.int32, (rows, LANES), 1)


def row_ids(rows):
    return lax.broadcasted_iota(jnp.int32, (rows, LANES), 0)


def dot_nt(a, b):
    return lax.dot_general(a, b, (((1,), (1,)), ((), ())), preferred_element_type=F32)


def sum_parts(stacked):
    rows = stacked.shape[0] // 3
    return stacked[:rows] + stacked[rows : 2 * rows] + stacked[2 * rows :]


def dot_nn(a, b):
    return lax.dot_general(a, b, (((1,), (0,)), ((), ())), preferred_element_type=F32)


def make_messages(tiles, air_ref, tile_ref, source_ref, cell_ref, weight_ref, msg_ref):
    count, air_cells = air_ref.shape
    chunks = tile_ref.shape[0]
    one, zero = jnp.ones((), F32), jnp.zeros((), F32)
    rows = [slice(c, c + 1) for c in range(chunks)]
    owns = [
        jnp.broadcast_to(tile_ref[r, :], (tiles, LANES)) == row_ids(tiles) for r in rows
    ]
    owned = jnp.concatenate([jnp.where(o, one, zero) for o in owns], axis=0).astype(jnp.bfloat16)
    earlier = jnp.where(row_ids(LANES) < lane_ids(LANES), one, zero).astype(jnp.bfloat16)
    prior = dot_nn(owned, earlier)
    total = dot_nn(owned, jnp.ones((LANES, LANES), jnp.bfloat16))
    air_parts = jnp.concatenate(
        [p.astype(F32) for p in thirds(air_ref[...])], axis=0
    ).astype(jnp.bfloat16)
    carry = jnp.zeros((tiles, LANES), F32)
    slots, parts = [], []
    for c in range(chunks):
        span = slice(c * tiles, (c + 1) * tiles)
        slots.append(
            jnp.sum(jnp.where(owns[c], prior[span] + carry, zero), axis=0, keepdims=True)
        )
        carry = carry + total[span]
        picked = jnp.broadcast_to(source_ref[rows[c], :], (air_cells, LANES)) == row_ids(air_cells)
        taken = dot_nn(air_parts, jnp.where(picked, one, zero).astype(jnp.bfloat16))
        flux = taken[:count] + taken[count : 2 * count] + taken[2 * count : 3 * count]
        payload = weight_ref[rows[c], :] * flux
        record = jnp.concatenate(
            [
                payload,
                cell_ref[rows[c], :].astype(F32),
                jnp.zeros((HALF - count - 1, LANES), F32),
            ],
            axis=0,
        )
        parts.append([p.astype(F32) for p in thirds(record)])
    slot_hot = jnp.concatenate(
        [
            jnp.where(
                jnp.broadcast_to(s.astype(jnp.int32), (LANES, LANES)) == row_ids(LANES), one, zero
            ).astype(jnp.bfloat16)
            for s in slots
        ],
        axis=1,
    )
    spread = jnp.concatenate(
        [
            jnp.concatenate(
                [
                    jnp.where(
                        jnp.broadcast_to(tile_ref[rows[c], :], (HALF, LANES)) == d,
                        parts[c][part],
                        zero,
                    )
                    for part in range(3)
                    for d in range(tiles)
                ],
                axis=0,
            ).astype(jnp.bfloat16)
            for c in range(chunks)
        ],
        axis=1,
    )
    out = sum_parts(dot_nt(spread, slot_hot))
    cells = pltpu.roll(pltpu.roll(out, CAP, 1).reshape(tiles, HALF, LANES), HALF - count, 1)
    out = out.reshape(tiles, HALF, LANES)
    head = lax.broadcasted_iota(jnp.int32, out.shape, 1) == 0
    msg_ref[...] = jnp.where(head, out + cells, out)[:, :count]


def pack_kernel(
    levels,
    tiles,
    tracer_hbm,
    east_hbm,
    north_hbm,
    kappa_hbm,
    depth_hbm,
    air_hbm,
    tile_hbm,
    source_hbm,
    cell_hbm,
    weight_hbm,
    up_ref,
    down_ref,
    mirror_ref,
    msg_ref,
    own_ref,
    tracer_ref,
    east_ref,
    north_ref,
    kappa_ref,
    depth_ref,
    air_ref,
    tile_ref,
    source_ref,
    cell_ref,
    weight_ref,
    sems,
    small_sems,
):
    count, _, cells, _ = tracer_ref.shape
    fields = count + 2
    chunk = chunk_of(levels)
    blocks = levels // chunk
    lane = lane_ids(cells)

    def copies(block):
        span = pl.ds(block * chunk, chunk)
        pairs = [
            (tracer_hbm.at[:, span], tracer_ref.at[:, span]),
            (north_hbm.at[span], north_ref.at[span]),
            (kappa_hbm.at[span], kappa_ref.at[span]),
            (east_hbm.at[span, pl.ds(cells - HALF, HALF)], east_ref.at[span]),
        ]
        return [
            pltpu.make_async_copy(src, dst, sems.at[block, i]) for i, (src, dst) in enumerate(pairs)
        ]

    small = [
        pltpu.make_async_copy(src, dst, small_sems.at[i])
        for i, (src, dst) in enumerate(
            (
                (tile_hbm, tile_ref),
                (air_hbm, air_ref),
                (source_hbm, source_ref),
                (cell_hbm, cell_ref),
                (weight_hbm, weight_ref),
                (depth_hbm, depth_ref),
            )
        )
    ]
    for copy in small:
        copy.start()
    for block in range(PACK_AHEAD):
        for copy in copies(block):
            copy.start()
    for copy in small:
        copy.wait()
    for block in range(PACK_AHEAD, blocks):
        for copy in copies(block):
            copy.start()

    depth = depth_ref[...].astype(F32)
    up_ref[fields * levels : fields * levels + 1, :] = depth[cells - 1 : cells]
    down_ref[(fields - 1) * levels : (fields - 1) * levels + 1, :] = depth[0:1]
    def several(group, columns):
        columns = list(columns)
        for inner in range(chunk):
            k = group * chunk + inner
            slabs = [tracer_ref[n, k] for n in range(count)] + [north_ref[k], kappa_ref[k]]
            for f in range(fields):
                columns[f] = jnp.where(lane == k, pltpu.roll(slabs[f], k + 1, 1), columns[f])
                if f < count:
                    up_ref[pl.ds(f * levels + k, 1), :] = slabs[f][cells - 1 : cells]
                    down_ref[pl.ds(f * levels + k, 1), :] = slabs[f][0:1]
            up_ref[pl.ds(count * levels + k, 1), :] = east_ref[k, HALF - 1 : HALF, :]
            up_ref[pl.ds((count + 1) * levels + k, 1), :] = slabs[count + 1][cells - 1 : cells]
            down_ref[pl.ds(count * levels + k, 1), :] = slabs[count + 1][0:1]
        return tuple(columns)

    columns = [jnp.zeros((cells, LANES), F32)] * fields
    for block in range(blocks):
        for copy in copies(block):
            copy.wait()
        if block == 0:
            make_messages(tiles, air_ref, tile_ref, source_ref, cell_ref, weight_ref, msg_ref)
        columns = several(block, columns)
    last = depth.shape[1] - 1
    columns = [*columns, jnp.broadcast_to(depth[:, last : last + 1], (cells, LANES))]
    for f in range(fields + 1):
        own_ref[f * cells : (f + 1) * cells, :] = columns[f]
        for i in range(cells):
            spot = f * cells + cells - 1 - i
            mirror_ref[spot : spot + 1, :] = columns[f][i : i + 1]


def pack(tiles, fields, small):
    count, levels, cells, lat = fields[0].shape
    rows = lambda n: jax.ShapeDtypeStruct((-(-n // HALF) * HALF, lat), F32)
    return pl.pallas_call(
        functools.partial(pack_kernel, levels, tiles),
        out_shape=[
            rows((count + 2) * levels + 1),
            rows((count + 1) * levels + 1),
            jax.ShapeDtypeStruct(((count + 3) * cells, LANES), F32),
            jax.ShapeDtypeStruct((tiles, count, LANES), F32),
            pltpu.HBM(((count + 3) * cells, LANES), F32),
        ],
        in_specs=[ANY] * (len(fields) + len(small)),
        out_specs=[VMEM] * 5,
        scratch_shapes=[
            pltpu.VMEM((count, levels, cells, lat), F32),
            pltpu.VMEM((levels, HALF, lat), F32),
            pltpu.VMEM((levels, cells, lat), F32),
            pltpu.VMEM((levels, cells, lat), F32),
        ]
        + [pltpu.VMEM(x.shape, x.dtype) for x in small]
        + [
            pltpu.SemaphoreType.DMA((levels // chunk_of(levels), 4)),
            pltpu.SemaphoreType.DMA((6,)),
        ],
        compiler_params=pltpu.CompilerParams(vmem_limit_bytes=12 << 20),
        cost_estimate=pl.CostEstimate(flops=10**7, bytes_accessed=4 * 10**6, transcendentals=0),
        name="pack",
    )(*in_hbm(*fields, *small))


def gather_surface(count, cells, lat, received_ref):
    tiles = received_ref.shape[0]
    shift = lat.bit_length() - 1
    one, zero = jnp.ones((), F32), jnp.zeros((), F32)
    left, right = [[], [], []], []
    early = lane_ids(count) < CAP
    for t in range(0, tiles, 2):
        even, odd = received_ref[t], received_ref[t + 1]
        block = jnp.where(early, even, pltpu.roll(odd, CAP, 1))
        cell = jnp.where(early, pltpu.roll(even, CAP, 1), odd)[0:1].astype(jnp.int32)
        row = jnp.broadcast_to(lax.shift_right_logical(cell, shift), (cells, LANES))
        col = jnp.broadcast_to(cell & (lat - 1), (lat, LANES))
        right.append(jnp.where(col == row_ids(lat), one, zero).astype(jnp.bfloat16))
        hit = row == row_ids(cells)
        for p, part in enumerate(thirds(block)):
            part = part.astype(F32)
            left[p].append(
                jnp.concatenate(
                    [
                        jnp.where(hit, jnp.broadcast_to(part[n : n + 1], (cells, LANES)), zero)
                        for n in range(count)
                    ],
                    axis=0,
                ).astype(jnp.bfloat16)
            )
    spread = jnp.concatenate(right, axis=1)
    parts = jnp.concatenate([jnp.concatenate(part, axis=1) for part in left], axis=0)
    return sum_parts(dot_nt(parts, spread))


def eliminate_kernel(
    levels,
    west_ref,
    far_ref,
    own_hbm,
    mirror_hbm,
    depth_hbm,
    tracer_hbm,
    kappa_hbm,
    north_hbm,
    east_hbm,
    thick_hbm,
    mixing_hbm,
    state_ref,
    own_ref,
    mirror_ref,
    depth_ref,
    tracer_ref,
    kappa_ref,
    north_ref,
    east_ref,
    thick_ref,
    mixing_ref,
    fold_ref,
    next_even,
    next_odd,
    part_even,
    part_odd,
    south_even,
    south_odd,
    small_sems,
    sems,
):
    count, _, cells, lat = tracer_ref.shape
    chunk = chunk_of(levels)
    blocks, groups = levels // chunk, chunk // GROUP

    def copies(block):
        span = pl.ds(block * chunk, chunk)
        pairs = [(tracer_hbm.at[:, span], tracer_ref.at[:, span])] + [
            (hbm.at[span], ref.at[span])
            for hbm, ref in (
                (kappa_hbm, kappa_ref),
                (north_hbm, north_ref),
                (east_hbm, east_ref),
                (thick_hbm, thick_ref),
                (mixing_hbm, mixing_ref),
            )
        ]
        return [
            pltpu.make_async_copy(src, dst, sems.at[block, i]) for i, (src, dst) in enumerate(pairs)
        ]

    def fetched(block):
        for copy in copies(block):
            copy.wait()

        @pl.when(block >= sum(AHEAD))
        def _():
            for copy in copies(block - sum(AHEAD)):
                copy.start()

    def begin(stage):
        done = sum(AHEAD[:stage])
        for block in range(done, done + AHEAD[stage]):
            for copy in copies(blocks - 1 - block):
                copy.start()

    small = [
        pltpu.make_async_copy(src, dst, small_sems.at[i])
        for i, (src, dst) in enumerate(
            ((own_hbm, own_ref), (mirror_hbm, mirror_ref), (depth_hbm, depth_ref))
        )
    ]
    for copy in small:
        copy.start()
    begin(0)
    halves = cells // HALF
    fields = count + 2
    row8 = row_ids(HALF)
    lane8 = lane_ids(HALF)
    top = lane8 == lat - 1
    first = row8 == 0
    last = row8 == HALF - 1
    hs = [slice(h * HALF, (h + 1) * HALF) for h in range(halves)]

    def from_east(parts, halo):
        turned = [pltpu.roll(p, HALF - 1, 0) for p in parts]
        return [
            jnp.where(last, turned[h + 1] if h + 1 < halves else halo, turned[h])
            for h in range(halves)
        ]

    def from_west(parts, halo):
        turned = [pltpu.roll(p, 1, 0) for p in parts]
        return [
            jnp.where(first, turned[h - 1] if h > 0 else halo, turned[h]) for h in range(halves)
        ]

    def row_of(ref, index):
        return jnp.broadcast_to(ref[pl.ds(index, 1), :], (HALF, lat))

    for copy in small:
        copy.wait()
    begin(1)
    for h in range(halves):
        mine, other = [
            [ref[f * cells + h * HALF : f * cells + (h + 1) * HALF, :] for f in range(fields + 1)]
            for ref in (own_ref, mirror_ref)
        ]
        mean = 0.5 * (mine[count + 1] + other[count + 1])
        speed = 0.5 * (mine[count] - other[count])
        open_face = jnp.minimum(mine[fields], other[fields]) > lane8.astype(F32)
        near = jnp.where(open_face, jnp.maximum(speed, 0.0) + mean, 0.0)
        far = jnp.where(open_face, jnp.minimum(speed, 0.0) - mean, 0.0)
        for n in range(count):
            flux = near * mine[n] + far * other[n]
            for k in range(levels):
                fold_ref[k, n, hs[h], :] = pltpu.roll(flux, lat - 1 - k, 1)
    begin(2)
    depth = [depth_ref[s, :].astype(F32) for s in hs]
    depth_east = from_east(depth, row_of(far_ref, (fields - 1) * levels))
    limit_here = depth
    limit_east = [jnp.minimum(depth[h], depth_east[h]) for h in range(halves)]
    limit_north = [
        jnp.where(top, 0.0, jnp.minimum(depth[h], pltpu.roll(depth[h], lat - 1, 1)))
        for h in range(halves)
    ]
    limit_west = jnp.minimum(
        jnp.broadcast_to(depth[0][0:1], (HALF, lat)), row_of(west_ref, fields * levels)
    )

    nexts, parts, souths = (next_even, next_odd), (part_even, part_odd), (south_even, south_odd)

    def turned(group, ring):
        next_ref = nexts[ring]
        for inner in range(GROUP):
            k = (levels - GROUP - group * GROUP) + (GROUP - 1 - inner)
            for s in hs:
                next_ref[inner, count, s, :] = pltpu.roll(kappa_ref[k, s, :], lat - 1, 1)
                for n in range(count):
                    next_ref[inner, n, s, :] = pltpu.roll(tracer_ref[n, k, s, :], lat - 1, 1)

    def fluxes(group, ring):
        next_ref, part_ref, south_ref = nexts[ring], parts[ring], souths[ring]
        for inner in range(GROUP):
            k = (levels - GROUP - group * GROUP) + (GROUP - 1 - inner)
            level = k.astype(F32)
            kappa = [kappa_ref[k, s, :] for s in hs]
            speed = [east_ref[k, s, :] for s in hs]
            kappa_east = from_east(kappa, row_of(far_ref, count * levels + k))
            near_e, far_e = [], []
            for h in range(halves):
                mean = 0.5 * (kappa[h] + kappa_east[h])
                open_face = limit_east[h] > level
                near = jnp.maximum(speed[h], 0.0) + mean
                near_e.append(jnp.where(open_face, near, 0.0))
                far_e.append(jnp.where(open_face, speed[h] - near, 0.0))
            speed_w = row_of(west_ref, count * levels + k)
            kappa_w = row_of(west_ref, (count + 1) * levels + k)
            mean = 0.5 * (kappa_w + jnp.broadcast_to(kappa[0][0:1], (HALF, lat)))
            open_face = limit_west > level
            near = jnp.maximum(speed_w, 0.0) + mean
            near_w = jnp.where(open_face, near, 0.0)
            far_w = jnp.where(open_face, speed_w - near, 0.0)
            near_n, far_n = [], []
            for h in range(halves):
                speed_n = north_ref[k, hs[h], :]
                mean = 0.5 * (kappa[h] + next_ref[inner, count, hs[h], :])
                open_face = limit_north[h] > level
                near = jnp.maximum(speed_n, 0.0) + mean
                near_n.append(jnp.where(open_face, near, 0.0))
                far_n.append(jnp.where(open_face, speed_n - near, 0.0))
            for n in range(count):
                cell = [tracer_ref[n, k, s, :] for s in hs]
                cell_east = from_east(cell, row_of(far_ref, n * levels + k))
                flux_e = [near_e[h] * cell[h] + far_e[h] * cell_east[h] for h in range(halves)]
                flux_in = near_w * row_of(west_ref, n * levels + k) + far_w * jnp.broadcast_to(
                    cell[0][0:1], (HALF, lat)
                )
                flux_w = from_west(flux_e, flux_in)
                for h in range(halves):
                    flux_n = near_n[h] * cell[h] + far_n[h] * next_ref[inner, n, hs[h], :]
                    south_ref[inner, n, hs[h], :] = pltpu.roll(flux_n, 1, 1)
                    flux_n = jnp.where(top, fold_ref[k, n, hs[h], :], flux_n)
                    part_ref[inner, n, hs[h], :] = (cell[h] - (flux_e[h] - flux_w[h])) - flux_n

    def solve(group, state, ring):
        part_ref, south_ref = parts[ring], souths[ring]
        thick, coupling, value, gain, scale = jax.tree.map(lambda x: x, state)
        for inner in range(GROUP):
            k = (levels - GROUP - group * GROUP) + (GROUP - 1 - inner)
            above = jnp.maximum(k - 1, 0)
            closed = jnp.where(k > 0, k.astype(F32), float(levels))
            for h in range(halves):
                thick_above = thick_ref[above, hs[h], :]
                here = 2.0 * mixing_ref[above, hs[h], :] / (thick_above + thick[h])
                here = jnp.where(limit_here[h] > closed, here, 0.0)
                scale[h] = 1.0 / (thick[h] + here + coupling[h] - coupling[h] * gain[h])
                gain[h] = here * scale[h]
                state_ref[count * levels + k, hs[h], :] = gain[h]
                share, below = thick[h] * scale[h], coupling[h] * scale[h]
                for n in range(count):
                    stepped = part_ref[inner, n, hs[h], :] + south_ref[inner, n, hs[h], :]
                    value[n][h] = share * stepped + below * value[n][h]
                    state_ref[n * levels + k, hs[h], :] = value[n][h]
                thick[h], coupling[h] = thick_above, here
        return thick, coupling, value, gain, scale

    def turn(group, state, ring):
        ahead = group + 1

        @pl.when(lax.rem(ahead, groups) == 0)
        def _():
            fetched(blocks - 1 - lax.div(ahead, groups))

        state = solve(group - 1, state, 1 - ring)
        turned(ahead, 1 - ring)
        fluxes(group, ring)
        return state

    def two_turns(pair, state):
        return turn(2 * pair + 2, turn(2 * pair + 1, state, 1), 0)

    zero = [jnp.zeros((HALF, lat), F32)] * halves
    total = blocks * groups
    fetched(jnp.int32(blocks - 1))
    turned(jnp.int32(0), 0)
    fluxes(jnp.int32(0), 0)
    turned(jnp.int32(1), 1)
    state = ([thick_ref[levels - 1, s, :] for s in hs], zero, [zero] * count, zero, zero)
    state = lax.fori_loop(0, (total - 2) // 2, two_turns, state)
    if total % 2:
        state = turn(jnp.int32(total - 2), state, 1)
    end = (total - 1) % 2
    fluxes(jnp.int32(total - 1), end)
    state = solve(jnp.int32(total - 2), state, 1 - end)
    scale = solve(jnp.int32(total - 1), state, end)[4]
    for h in range(halves):
        state_ref[count * levels, hs[h], :] = jnp.where(limit_here[h] > 0.0, scale[h], 0.0)


def substitute_kernel(state_ref, received_ref, out_hbm, out_ref, sems):
    count, levels, cells, lat = out_ref.shape
    chunk = chunk_of(levels)
    blocks = levels // chunk
    hs = [slice(h, h + HALF) for h in range(0, cells, HALF)]

    def result(block):
        span = pl.ds(block * chunk, chunk)
        return pltpu.make_async_copy(out_ref.at[:, span], out_hbm.at[:, span], sems.at[block])

    surface = gather_surface(count, cells, lat, received_ref)
    solved = [[surface[n * cells + s.start : n * cells + s.stop] for s in hs] for n in range(count)]

    def descend(group, solved):
        solved = jax.tree.map(lambda x: x, solved)
        for inner in range(GROUP):
            k = group * GROUP + inner
            for h, s in enumerate(hs):
                gain = state_ref[count * levels + k, s, :]
                for n in range(count):
                    solved[n][h] = state_ref[n * levels + k, s, :] + gain * solved[n][h]
                    out_ref[n, k, s, :] = solved[n][h]
        return solved

    def substitute(block, solved):
        first = block * (chunk // GROUP)
        solved = lax.fori_loop(first, first + chunk // GROUP, descend, solved)
        result(block).start()
        return solved

    lax.fori_loop(0, blocks, substitute, solved)
    for block in range(blocks):
        result(block).wait()


def eliminate(halos, small, fields):
    count, levels, cells, lat = fields[0].shape
    return pl.pallas_call(
        functools.partial(eliminate_kernel, levels),
        out_shape=pltpu.VMEM(((count + 1) * levels, cells, lat), F32),
        in_specs=[VMEM] * len(halos) + [ANY] * (len(small) + len(fields)),
        out_specs=VMEM,
        scratch_shapes=[pltpu.VMEM(x.shape, x.dtype) for x in (*small, *fields)]
        + [
            pltpu.VMEM((levels, count, cells, lat), F32),
            pltpu.VMEM((GROUP, count + 1, cells, lat), F32),
            pltpu.VMEM((GROUP, count + 1, cells, lat), F32),
        ]
        + [pltpu.VMEM((GROUP, count, cells, lat), F32)] * 4
        + [
            pltpu.SemaphoreType.DMA((len(small),)),
            pltpu.SemaphoreType.DMA((levels // chunk_of(levels), len(fields))),
        ],
        compiler_params=pltpu.CompilerParams(vmem_limit_bytes=16 << 20),
        cost_estimate=pl.CostEstimate(flops=10**8, bytes_accessed=8 * 10**6, transcendentals=0),
        name="eliminate",
    )(*in_vmem(*halos), *in_hbm(*small, *fields))


def settle_kernel(block_ref, out_hbm, sem):
    copy = pltpu.make_async_copy(block_ref, out_hbm, sem)
    copy.start()
    copy.wait()


def settle(block):
    return pl.pallas_call(
        settle_kernel,
        out_shape=pltpu.HBM(block.shape, block.dtype),
        in_specs=[VMEM],
        out_specs=ANY,
        scratch_shapes=[pltpu.SemaphoreType.DMA],
        cost_estimate=pl.CostEstimate(flops=SETTLE, bytes_accessed=10**5, transcendentals=0),
        name="settle",
    )(*in_vmem(block))


def substitute(count, levels, state, received):
    shape = (count, levels, *state.shape[1:])
    return pl.pallas_call(
        substitute_kernel,
        out_shape=jax.ShapeDtypeStruct(shape, F32),
        in_specs=[VMEM] * 2,
        out_specs=ANY,
        scratch_shapes=[
            pltpu.VMEM(shape, F32),
            pltpu.SemaphoreType.DMA((levels // chunk_of(levels),)),
        ],
        compiler_params=pltpu.CompilerParams(vmem_limit_bytes=12 << 20),
        cost_estimate=pl.CostEstimate(flops=10**7, bytes_accessed=6 * 10**6, transcendentals=0),
        name="substitute",
    )(*in_vmem(state, received))


def shards(
    tracer,
    east_speed,
    north_speed,
    diffusivity,
    mixing,
    thickness,
    depth_levels,
    air_flux,
    margin_tile,
    margin_source,
    margin_cell,
    margin_weight,
):
    tiles = lax.axis_size("lon")
    by_level = lambda x: jnp.transpose(x, (1, 0, 2))
    rows = lambda x: x.reshape(-1, LANES)
    tracer = jnp.transpose(tracer, (0, 2, 1, 3))
    east, north, kappa, mixing, thick = [
        by_level(x) for x in (east_speed, north_speed, diffusivity, mixing, thickness)
    ]
    count, levels = tracer.shape[:2]
    small = [depth_levels, air_flux]
    small += [rows(x) for x in (margin_tile, margin_source, margin_cell, margin_weight)]
    up, down, mirror, messages, own = pack(tiles, [tracer, east, north, kappa], small)
    ring = [(i, (i + 1) % tiles) for i in range(tiles)]
    mirror = lax.ppermute(mirror, "lon", [(i, tiles - 1 - i) for i in range(tiles)])
    west = lax.ppermute(up, "lon", ring)
    far = lax.ppermute(down, "lon", [(j, i) for i, j in ring])
    received = lax.all_to_all(messages, "lon", split_axis=0, concat_axis=0, tiled=True)
    mirror = settle(mirror)
    fields = [tracer, kappa, north, east, thick, mixing]
    state = eliminate([west, far], [own, mirror, depth_levels], fields)
    out = substitute(count, levels, state, received)
    return jnp.transpose(out, (0, 2, 1, 3))


def solution(mesh):
    placed = (
        P(None, "lon", None, "ens"),
        P("lon", None, "ens"),
        P("lon", None, "ens"),
        P("lon", None, "ens"),
        P("lon", None, "ens"),
        P("lon", None, "ens"),
        P("lon", "ens"),
        P("ens", "lon"),
        P(("ens", "lon"), None),
        P(("ens", "lon")),
        P(("ens", "lon")),
        P(("ens", "lon")),
    )
    return jax.shard_map(
        shards, mesh=mesh, in_specs=placed, out_specs=P(None, "lon", None, "ens"), check_vma=False
    )
```

```python
import functools

import jax
import jax.numpy as jnp
from jax import lax
from jax.experimental import pallas as pl
from jax.experimental.pallas import tpu as pltpu
from jax.sharding import PartitionSpec as P

CAP = 64
HALF = 8
GROUP = 5
AHEAD = (2, 1, 0)
PACK_AHEAD = 2
SETTLE = 17 * 10**8
LANES = 128
F32 = jnp.float32


def chunk_of(levels):
    return max(c for c in range(GROUP, 4 * GROUP, GROUP) if levels % c == 0)


def thirds(x):
    high = x.astype(jnp.bfloat16)
    rest = x - high.astype(F32)
    mid = rest.astype(jnp.bfloat16)
    low = (rest - mid.astype(F32)).astype(jnp.bfloat16)
    return high, mid, low


VMEM = pl.BlockSpec(memory_space=pltpu.VMEM)
ANY = pl.BlockSpec(memory_space=pl.ANY)


def in_hbm(*arrays):
    return [pltpu.with_memory_space_constraint(x, pltpu.HBM) for x in arrays]


def in_vmem(*arrays):
    return [pltpu.with_memory_space_constraint(x, pltpu.VMEM) for x in arrays]


def lane_ids(rows):
    return lax.broadcasted_iota(jnp.int32, (rows, LANES), 1)


def row_ids(rows):
    return lax.broadcasted_iota(jnp.int32, (rows, LANES), 0)


def dot_nt(a, b):
    return lax.dot_general(a, b, (((1,), (1,)), ((), ())), preferred_element_type=F32)


def sum_parts(stacked):
    rows = stacked.shape[0] // 3
    return stacked[:rows] + stacked[rows : 2 * rows] + stacked[2 * rows :]


def dot_nn(a, b):
    return lax.dot_general(a, b, (((1,), (0,)), ((), ())), preferred_element_type=F32)


def make_messages(tiles, air_ref, tile_ref, source_ref, cell_ref, weight_ref, msg_ref):
    count, air_cells = air_ref.shape
    chunks = tile_ref.shape[0]
    one, zero = jnp.ones((), F32), jnp.zeros((), F32)
    rows = [slice(c, c + 1) for c in range(chunks)]
    owns = [
        jnp.broadcast_to(tile_ref[r, :], (tiles, LANES)) == row_ids(tiles) for r in rows
    ]
    owned = jnp.concatenate([jnp.where(o, one, zero) for o in owns], axis=0).astype(jnp.bfloat16)
    earlier = jnp.where(row_ids(LANES) < lane_ids(LANES), one, zero).astype(jnp.bfloat16)
    prior = dot_nn(owned, earlier)
    total = dot_nn(owned, jnp.ones((LANES, LANES), jnp.bfloat16))
    air_parts = jnp.concatenate(
        [p.astype(F32) for p in thirds(air_ref[...])], axis=0
    ).astype(jnp.bfloat16)
    carry = jnp.zeros((tiles, LANES), F32)
    slots, parts = [], []
    for c in range(chunks):
        span = slice(c * tiles, (c + 1) * tiles)
        slots.append(
            jnp.sum(jnp.where(owns[c], prior[span] + carry, zero), axis=0, keepdims=True)
        )
        carry = carry + total[span]
        picked = jnp.broadcast_to(source_ref[rows[c], :], (air_cells, LANES)) == row_ids(air_cells)
        taken = dot_nn(air_parts, jnp.where(picked, one, zero).astype(jnp.bfloat16))
        flux = taken[:count] + taken[count : 2 * count] + taken[2 * count : 3 * count]
        payload = weight_ref[rows[c], :] * flux
        record = jnp.concatenate(
            [
                payload,
                cell_ref[rows[c], :].astype(F32),
                jnp.zeros((HALF - count - 1, LANES), F32),
            ],
            axis=0,
        )
        parts.append([p.astype(F32) for p in thirds(record)])
    slot_hot = jnp.concatenate(
        [
            jnp.where(
                jnp.broadcast_to(s.astype(jnp.int32), (LANES, LANES)) == row_ids(LANES), one, zero
            ).astype(jnp.bfloat16)
            for s in slots
        ],
        axis=1,
    )
    spread = jnp.concatenate(
        [
            jnp.concatenate(
                [
                    jnp.where(
                        jnp.broadcast_to(tile_ref[rows[c], :], (HALF, LANES)) == d,
                        parts[c][part],
                        zero,
                    )
                    for part in range(3)
                    for d in range(tiles)
                ],
                axis=0,
            ).astype(jnp.bfloat16)
            for c in range(chunks)
        ],
        axis=1,
    )
    out = sum_parts(dot_nt(spread, slot_hot))
    cells = pltpu.roll(pltpu.roll(out, CAP, 1).reshape(tiles, HALF, LANES), HALF - count, 1)
    out = out.reshape(tiles, HALF, LANES)
    head = lax.broadcasted_iota(jnp.int32, out.shape, 1) == 0
    msg_ref[...] = jnp.where(head, out + cells, out)[:, :count]


def pack_kernel(
    levels,
    tiles,
    tracer_hbm,
    east_hbm,
    north_hbm,
    kappa_hbm,
    depth_hbm,
    air_hbm,
    tile_hbm,
    source_hbm,
    cell_hbm,
    weight_hbm,
    up_ref,
    down_ref,
    mirror_ref,
    msg_ref,
    own_ref,
    tracer_ref,
    east_ref,
    north_ref,
    kappa_ref,
    depth_ref,
    air_ref,
    tile_ref,
    source_ref,
    cell_ref,
    weight_ref,
    sems,
    small_sems,
):
    count, _, cells, _ = tracer_ref.shape
    fields = count + 2
    chunk = chunk_of(levels)
    blocks = levels // chunk
    lane = lane_ids(cells)

    def copies(block):
        span = pl.ds(block * chunk, chunk)
        pairs = [
            (tracer_hbm.at[:, span], tracer_ref.at[:, span]),
            (north_hbm.at[span], north_ref.at[span]),
            (kappa_hbm.at[span], kappa_ref.at[span]),
            (east_hbm.at[span, pl.ds(cells - HALF, HALF)], east_ref.at[span]),
        ]
        return [
            pltpu.make_async_copy(src, dst, sems.at[block, i]) for i, (src, dst) in enumerate(pairs)
        ]

    small = [
        pltpu.make_async_copy(src, dst, small_sems.at[i])
        for i, (src, dst) in enumerate(
            (
                (tile_hbm, tile_ref),
                (air_hbm, air_ref),
                (source_hbm, source_ref),
                (cell_hbm, cell_ref),
                (weight_hbm, weight_ref),
                (depth_hbm, depth_ref),
            )
        )
    ]
    for copy in small:
        copy.start()
    for block in range(PACK_AHEAD):
        for copy in copies(block):
            copy.start()
    for copy in small:
        copy.wait()
    for block in range(PACK_AHEAD, blocks):
        for copy in copies(block):
            copy.start()

    depth = depth_ref[...].astype(F32)
    up_ref[fields * levels : fields * levels + 1, :] = depth[cells - 1 : cells]
    down_ref[(fields - 1) * levels : (fields - 1) * levels + 1, :] = depth[0:1]
    def several(group, columns):
        columns = list(columns)
        for inner in range(chunk):
            k = group * chunk + inner
            slabs = [tracer_ref[n, k] for n in range(count)] + [north_ref[k], kappa_ref[k]]
            for f in range(fields):
                columns[f] = jnp.where(lane == k, pltpu.roll(slabs[f], k + 1, 1), columns[f])
                if f < count:
                    up_ref[pl.ds(f * levels + k, 1), :] = slabs[f][cells - 1 : cells]
                    down_ref[pl.ds(f * levels + k, 1), :] = slabs[f][0:1]
            up_ref[pl.ds(count * levels + k, 1), :] = east_ref[k, HALF - 1 : HALF, :]
            up_ref[pl.ds((count + 1) * levels + k, 1), :] = slabs[count + 1][cells - 1 : cells]
            down_ref[pl.ds(count * levels + k, 1), :] = slabs[count + 1][0:1]
        return tuple(columns)

    columns = [jnp.zeros((cells, LANES), F32)] * fields
    for block in range(blocks):
        for copy in copies(block):
            copy.wait()
        if block == 0:
            make_messages(tiles, air_ref, tile_ref, source_ref, cell_ref, weight_ref, msg_ref)
        columns = several(block, columns)
    last = depth.shape[1] - 1
    columns = [*columns, jnp.broadcast_to(depth[:, last : last + 1], (cells, LANES))]
    for f in range(fields + 1):
        own_ref[f * cells : (f + 1) * cells, :] = columns[f]
        for i in range(cells):
            spot = f * cells + cells - 1 - i
            mirror_ref[spot : spot + 1, :] = columns[f][i : i + 1]


def pack(tiles, fields, small):
    count, levels, cells, lat = fields[0].shape
    rows = lambda n: jax.ShapeDtypeStruct((-(-n // HALF) * HALF, lat), F32)
    return pl.pallas_call(
        functools.partial(pack_kernel, levels, tiles),
        out_shape=[
            rows((count + 2) * levels + 1),
            rows((count + 1) * levels + 1),
            jax.ShapeDtypeStruct(((count + 3) * cells, LANES), F32),
            jax.ShapeDtypeStruct((tiles, count, LANES), F32),
            pltpu.HBM(((count + 3) * cells, LANES), F32),
        ],
        in_specs=[ANY] * (len(fields) + len(small)),
        out_specs=[VMEM] * 5,
        scratch_shapes=[
            pltpu.VMEM((count, levels, cells, lat), F32),
            pltpu.VMEM((levels, HALF, lat), F32),
            pltpu.VMEM((levels, cells, lat), F32),
            pltpu.VMEM((levels, cells, lat), F32),
        ]
        + [pltpu.VMEM(x.shape, x.dtype) for x in small]
        + [
            pltpu.SemaphoreType.DMA((levels // chunk_of(levels), 4)),
            pltpu.SemaphoreType.DMA((6,)),
        ],
        compiler_params=pltpu.CompilerParams(vmem_limit_bytes=12 << 20),
        cost_estimate=pl.CostEstimate(flops=10**7, bytes_accessed=4 * 10**6, transcendentals=0),
        name="pack",
    )(*in_hbm(*fields, *small))


def gather_surface(count, cells, lat, received_ref):
    tiles = received_ref.shape[0]
    shift = lat.bit_length() - 1
    one, zero = jnp.ones((), F32), jnp.zeros((), F32)
    left, right = [[], [], []], []
    early = lane_ids(count) < CAP
    for t in range(0, tiles, 2):
        even, odd = received_ref[t], received_ref[t + 1]
        block = jnp.where(early, even, pltpu.roll(odd, CAP, 1))
        cell = jnp.where(early, pltpu.roll(even, CAP, 1), odd)[0:1].astype(jnp.int32)
        row = jnp.broadcast_to(lax.shift_right_logical(cell, shift), (cells, LANES))
        col = jnp.broadcast_to(cell & (lat - 1), (lat, LANES))
        right.append(jnp.where(col == row_ids(lat), one, zero).astype(jnp.bfloat16))
        hit = row == row_ids(cells)
        for p, part in enumerate(thirds(block)):
            part = part.astype(F32)
            left[p].append(
                jnp.concatenate(
                    [
                        jnp.where(hit, jnp.broadcast_to(part[n : n + 1], (cells, LANES)), zero)
                        for n in range(count)
                    ],
                    axis=0,
                ).astype(jnp.bfloat16)
            )
    spread = jnp.concatenate(right, axis=1)
    parts = jnp.concatenate([jnp.concatenate(part, axis=1) for part in left], axis=0)
    return sum_parts(dot_nt(parts, spread))


def eliminate_kernel(
    levels,
    west_ref,
    far_ref,
    own_hbm,
    mirror_hbm,
    depth_hbm,
    tracer_hbm,
    kappa_hbm,
    north_hbm,
    east_hbm,
    thick_hbm,
    mixing_hbm,
    state_ref,
    own_ref,
    mirror_ref,
    depth_ref,
    tracer_ref,
    kappa_ref,
    north_ref,
    east_ref,
    thick_ref,
    mixing_ref,
    fold_ref,
    next_even,
    next_odd,
    part_even,
    part_odd,
    south_even,
    south_odd,
    small_sems,
    sems,
):
    count, _, cells, lat = tracer_ref.shape
    chunk = chunk_of(levels)
    blocks, groups = levels // chunk, chunk // GROUP

    def copies(block):
        span = pl.ds(block * chunk, chunk)
        pairs = [(tracer_hbm.at[:, span], tracer_ref.at[:, span])] + [
            (hbm.at[span], ref.at[span])
            for hbm, ref in (
                (kappa_hbm, kappa_ref),
                (north_hbm, north_ref),
                (east_hbm, east_ref),
                (thick_hbm, thick_ref),
                (mixing_hbm, mixing_ref),
            )
        ]
        return [
            pltpu.make_async_copy(src, dst, sems.at[block, i]) for i, (src, dst) in enumerate(pairs)
        ]

    def fetched(block):
        for copy in copies(block):
            copy.wait()

        @pl.when(block >= sum(AHEAD))
        def _():
            for copy in copies(block - sum(AHEAD)):
                copy.start()

    def begin(stage):
        done = sum(AHEAD[:stage])
        for block in range(done, done + AHEAD[stage]):
            for copy in copies(blocks - 1 - block):
                copy.start()

    small = [
        pltpu.make_async_copy(src, dst, small_sems.at[i])
        for i, (src, dst) in enumerate(
            ((own_hbm, own_ref), (mirror_hbm, mirror_ref), (depth_hbm, depth_ref))
        )
    ]
    for copy in small:
        copy.start()
    begin(0)
    halves = cells // HALF
    fields = count + 2
    row8 = row_ids(HALF)
    lane8 = lane_ids(HALF)
    top = lane8 == lat - 1
    first = row8 == 0
    last = row8 == HALF - 1
    hs = [slice(h * HALF, (h + 1) * HALF) for h in range(halves)]

    def from_east(parts, halo):
        turned = [pltpu.roll(p, HALF - 1, 0) for p in parts]
        return [
            jnp.where(last, turned[h + 1] if h + 1 < halves else halo, turned[h])
            for h in range(halves)
        ]

    def from_west(parts, halo):
        turned = [pltpu.roll(p, 1, 0) for p in parts]
        return [
            jnp.where(first, turned[h - 1] if h > 0 else halo, turned[h]) for h in range(halves)
        ]

    def row_of(ref, index):
        return jnp.broadcast_to(ref[pl.ds(index, 1), :], (HALF, lat))

    for copy in small:
        copy.wait()
    begin(1)
    for h in range(halves):
        mine, other = [
            [ref[f * cells + h * HALF : f * cells + (h + 1) * HALF, :] for f in range(fields + 1)]
            for ref in (own_ref, mirror_ref)
        ]
        mean = 0.5 * (mine[count + 1] + other[count + 1])
        speed = 0.5 * (mine[count] - other[count])
        open_face = jnp.minimum(mine[fields], other[fields]) > lane8.astype(F32)
        near = jnp.where(open_face, jnp.maximum(speed, 0.0) + mean, 0.0)
        far = jnp.where(open_face, jnp.minimum(speed, 0.0) - mean, 0.0)
        for n in range(count):
            flux = near * mine[n] + far * other[n]
            for k in range(levels):
                fold_ref[k, n, hs[h], :] = pltpu.roll(flux, lat - 1 - k, 1)
    begin(2)
    depth = [depth_ref[s, :].astype(F32) for s in hs]
    depth_east = from_east(depth, row_of(far_ref, (fields - 1) * levels))
    limit_here = depth
    limit_east = [jnp.minimum(depth[h], depth_east[h]) for h in range(halves)]
    limit_north = [
        jnp.where(top, 0.0, jnp.minimum(depth[h], pltpu.roll(depth[h], lat - 1, 1)))
        for h in range(halves)
    ]
    limit_west = jnp.minimum(
        jnp.broadcast_to(depth[0][0:1], (HALF, lat)), row_of(west_ref, fields * levels)
    )

    nexts, parts, souths = (next_even, next_odd), (part_even, part_odd), (south_even, south_odd)

    def turned(group, ring):
        next_ref = nexts[ring]
        for inner in range(GROUP):
            k = (levels - GROUP - group * GROUP) + (GROUP - 1 - inner)
            for s in hs:
                kappa = kappa_ref[k, s, :]
                next_ref[inner, count, s, :] = 0.5 * (kappa + pltpu.roll(kappa, lat - 1, 1))
                for n in range(count):
                    next_ref[inner, n, s, :] = pltpu.roll(tracer_ref[n, k, s, :], lat - 1, 1)

    def fluxes(group, ring):
        next_ref, part_ref, south_ref = nexts[ring], parts[ring], souths[ring]
        for inner in range(GROUP):
            k = (levels - GROUP - group * GROUP) + (GROUP - 1 - inner)
            level = k.astype(F32)
            kappa = [kappa_ref[k, s, :] for s in hs]
            speed = [east_ref[k, s, :] for s in hs]
            kappa_east = from_east(kappa, row_of(far_ref, count * levels + k))
            near_e, far_e = [], []
            for h in range(halves):
                mean = 0.5 * (kappa[h] + kappa_east[h])
                open_face = limit_east[h] > level
                near = jnp.maximum(speed[h], 0.0) + mean
                near_e.append(jnp.where(open_face, near, 0.0))
                far_e.append(jnp.where(open_face, speed[h] - near, 0.0))
            speed_w = row_of(west_ref, count * levels + k)
            kappa_w = row_of(west_ref, (count + 1) * levels + k)
            mean = 0.5 * (kappa_w + jnp.broadcast_to(kappa[0][0:1], (HALF, lat)))
            open_face = limit_west > level
            near = jnp.maximum(speed_w, 0.0) + mean
            near_w = jnp.where(open_face, near, 0.0)
            far_w = jnp.where(open_face, speed_w - near, 0.0)
            near_n, far_n = [], []
            for h in range(halves):
                speed_n = north_ref[k, hs[h], :]
                mean = next_ref[inner, count, hs[h], :]
                open_face = limit_north[h] > level
                near = jnp.maximum(speed_n, 0.0) + mean
                near_n.append(jnp.where(open_face, near, 0.0))
                far_n.append(jnp.where(open_face, speed_n - near, 0.0))
            for n in range(count):
                cell = [tracer_ref[n, k, s, :] for s in hs]
                cell_east = from_east(cell, row_of(far_ref, n * levels + k))
                flux_e = [near_e[h] * cell[h] + far_e[h] * cell_east[h] for h in range(halves)]
                flux_in = near_w * row_of(west_ref, n * levels + k) + far_w * jnp.broadcast_to(
                    cell[0][0:1], (HALF, lat)
                )
                flux_w = from_west(flux_e, flux_in)
                for h in range(halves):
                    flux_n = near_n[h] * cell[h] + far_n[h] * next_ref[inner, n, hs[h], :]
                    south_ref[inner, n, hs[h], :] = pltpu.roll(flux_n, 1, 1)
                    flux_n = jnp.where(top, fold_ref[k, n, hs[h], :], flux_n)
                    part_ref[inner, n, hs[h], :] = (cell[h] - (flux_e[h] - flux_w[h])) - flux_n

    def solve(group, state, ring):
        part_ref, south_ref = parts[ring], souths[ring]
        thick, coupling, value, gain, scale = jax.tree.map(lambda x: x, state)
        for inner in range(GROUP):
            k = (levels - GROUP - group * GROUP) + (GROUP - 1 - inner)
            above = jnp.maximum(k - 1, 0)
            closed = jnp.where(k > 0, k.astype(F32), float(levels))
            for h in range(halves):
                thick_above = thick_ref[above, hs[h], :]
                here = 2.0 * mixing_ref[above, hs[h], :] / (thick_above + thick[h])
                here = jnp.where(limit_here[h] > closed, here, 0.0)
                scale[h] = 1.0 / (thick[h] + here + coupling[h] - coupling[h] * gain[h])
                gain[h] = here * scale[h]
                state_ref[count * levels + k, hs[h], :] = gain[h]
                share, below = thick[h] * scale[h], coupling[h] * scale[h]
                for n in range(count):
                    stepped = part_ref[inner, n, hs[h], :] + south_ref[inner, n, hs[h], :]
                    value[n][h] = share * stepped + below * value[n][h]
                    state_ref[n * levels + k, hs[h], :] = value[n][h]
                thick[h], coupling[h] = thick_above, here
        return thick, coupling, value, gain, scale

    def turn(group, state, ring):
        ahead = group + 1

        @pl.when(lax.rem(ahead, groups) == 0)
        def _():
            fetched(blocks - 1 - lax.div(ahead, groups))

        state = solve(group - 1, state, 1 - ring)
        turned(ahead, 1 - ring)
        fluxes(group, ring)
        return state

    def two_turns(pair, state):
        return turn(2 * pair + 2, turn(2 * pair + 1, state, 1), 0)

    zero = [jnp.zeros((HALF, lat), F32)] * halves
    total = blocks * groups
    fetched(jnp.int32(blocks - 1))
    turned(jnp.int32(0), 0)
    fluxes(jnp.int32(0), 0)
    turned(jnp.int32(1), 1)
    state = ([thick_ref[levels - 1, s, :] for s in hs], zero, [zero] * count, zero, zero)
    state = lax.fori_loop(0, (total - 2) // 2, two_turns, state)
    if total % 2:
        state = turn(jnp.int32(total - 2), state, 1)
    end = (total - 1) % 2
    fluxes(jnp.int32(total - 1), end)
    state = solve(jnp.int32(total - 2), state, 1 - end)
    scale = solve(jnp.int32(total - 1), state, end)[4]
    for h in range(halves):
        state_ref[count * levels, hs[h], :] = jnp.where(limit_here[h] > 0.0, scale[h], 0.0)


def substitute_kernel(state_ref, received_ref, out_hbm, out_ref, sems):
    count, levels, cells, lat = out_ref.shape
    chunk = chunk_of(levels)
    blocks = levels // chunk
    hs = [slice(h, h + HALF) for h in range(0, cells, HALF)]

    def result(block):
        span = pl.ds(block * chunk, chunk)
        return pltpu.make_async_copy(out_ref.at[:, span], out_hbm.at[:, span], sems.at[block])

    surface = gather_surface(count, cells, lat, received_ref)
    solved = [[surface[n * cells + s.start : n * cells + s.stop] for s in hs] for n in range(count)]

    def descend(group, solved):
        solved = jax.tree.map(lambda x: x, solved)
        for inner in range(GROUP):
            k = group * GROUP + inner
            for h, s in enumerate(hs):
                gain = state_ref[count * levels + k, s, :]
                for n in range(count):
                    solved[n][h] = state_ref[n * levels + k, s, :] + gain * solved[n][h]
                    out_ref[n, k, s, :] = solved[n][h]
        return solved

    def substitute(block, solved):
        first = block * (chunk // GROUP)
        solved = lax.fori_loop(first, first + chunk // GROUP, descend, solved)
        result(block).start()
        return solved

    lax.fori_loop(0, blocks, substitute, solved)
    for block in range(blocks):
        result(block).wait()


def eliminate(halos, small, fields):
    count, levels, cells, lat = fields[0].shape
    return pl.pallas_call(
        functools.partial(eliminate_kernel, levels),
        out_shape=pltpu.VMEM(((count + 1) * levels, cells, lat), F32),
        in_specs=[VMEM] * len(halos) + [ANY] * (len(small) + len(fields)),
        out_specs=VMEM,
        scratch_shapes=[pltpu.VMEM(x.shape, x.dtype) for x in (*small, *fields)]
        + [
            pltpu.VMEM((levels, count, cells, lat), F32),
            pltpu.VMEM((GROUP, count + 1, cells, lat), F32),
            pltpu.VMEM((GROUP, count + 1, cells, lat), F32),
        ]
        + [pltpu.VMEM((GROUP, count, cells, lat), F32)] * 4
        + [
            pltpu.SemaphoreType.DMA((len(small),)),
            pltpu.SemaphoreType.DMA((levels // chunk_of(levels), len(fields))),
        ],
        compiler_params=pltpu.CompilerParams(vmem_limit_bytes=16 << 20),
        cost_estimate=pl.CostEstimate(flops=10**8, bytes_accessed=8 * 10**6, transcendentals=0),
        name="eliminate",
    )(*in_vmem(*halos), *in_hbm(*small, *fields))


def settle_kernel(block_ref, out_hbm, sem):
    copy = pltpu.make_async_copy(block_ref, out_hbm, sem)
    copy.start()
    copy.wait()


def settle(block):
    return pl.pallas_call(
        settle_kernel,
        out_shape=pltpu.HBM(block.shape, block.dtype),
        in_specs=[VMEM],
        out_specs=ANY,
        scratch_shapes=[pltpu.SemaphoreType.DMA],
        cost_estimate=pl.CostEstimate(flops=SETTLE, bytes_accessed=10**5, transcendentals=0),
        name="settle",
    )(*in_vmem(block))


def substitute(count, levels, state, received):
    shape = (count, levels, *state.shape[1:])
    return pl.pallas_call(
        substitute_kernel,
        out_shape=jax.ShapeDtypeStruct(shape, F32),
        in_specs=[VMEM] * 2,
        out_specs=ANY,
        scratch_shapes=[
            pltpu.VMEM(shape, F32),
            pltpu.SemaphoreType.DMA((levels // chunk_of(levels),)),
        ],
        compiler_params=pltpu.CompilerParams(vmem_limit_bytes=12 << 20),
        cost_estimate=pl.CostEstimate(flops=10**7, bytes_accessed=6 * 10**6, transcendentals=0),
        name="substitute",
    )(*in_vmem(state, received))


def shards(
    tracer,
    east_speed,
    north_speed,
    diffusivity,
    mixing,
    thickness,
    depth_levels,
    air_flux,
    margin_tile,
    margin_source,
    margin_cell,
    margin_weight,
):
    tiles = lax.axis_size("lon")
    by_level = lambda x: jnp.transpose(x, (1, 0, 2))
    rows = lambda x: x.reshape(-1, LANES)
    tracer = jnp.transpose(tracer, (0, 2, 1, 3))
    east, north, kappa, mixing, thick = [
        by_level(x) for x in (east_speed, north_speed, diffusivity, mixing, thickness)
    ]
    count, levels = tracer.shape[:2]
    small = [depth_levels, air_flux]
    small += [rows(x) for x in (margin_tile, margin_source, margin_cell, margin_weight)]
    up, down, mirror, messages, own = pack(tiles, [tracer, east, north, kappa], small)
    ring = [(i, (i + 1) % tiles) for i in range(tiles)]
    mirror = lax.ppermute(mirror, "lon", [(i, tiles - 1 - i) for i in range(tiles)])
    west = lax.ppermute(up, "lon", ring)
    far = lax.ppermute(down, "lon", [(j, i) for i, j in ring])
    received = lax.all_to_all(messages, "lon", split_axis=0, concat_axis=0, tiled=True)
    mirror = settle(mirror)
    fields = [tracer, kappa, north, east, thick, mixing]
    state = eliminate([west, far], [own, mirror, depth_levels], fields)
    out = substitute(count, levels, state, received)
    return jnp.transpose(out, (0, 2, 1, 3))


def solution(mesh):
    placed = (
        P(None, "lon", None, "ens"),
        P("lon", None, "ens"),
        P("lon", None, "ens"),
        P("lon", None, "ens"),
        P("lon", None, "ens"),
        P("lon", None, "ens"),
        P("lon", "ens"),
        P("ens", "lon"),
        P(("ens", "lon"), None),
        P(("ens", "lon")),
        P(("ens", "lon")),
        P(("ens", "lon")),
    )
    return jax.shard_map(
        shards, mesh=mesh, in_specs=placed, out_specs=P(None, "lon", None, "ens"), check_vma=False
    )
```
